32 devices in a mesh: section: 4 (over y, x), expert: 8 (over z, core).
Axes of the slice: x: 2, y: 2, z: 4, core: 2. Of those that a mesh axis runs over, the one named last changes fastest.
Arguments:
- tokens: bfloat16 [4, 128, 7168], P('section', 'expert'), may hold values from -6 to 6
- route_experts: int32 [4, 128, 2], P('section', 'expert'), may hold values from 0 to 3, as said below
- route_slots: int32 [4, 128, 2], P('section', 'expert'), may hold values from 0 to 15, as said below
- route_weights: float32 [4, 128, 2], P('section', 'expert'), may hold values from 0.1 to 1
- gate_weight: bfloat16 [4, 7168, 8192], P('section', None, 'expert'), may hold values from -0.0625 to 0.0625
- up_weight: bfloat16 [4, 7168, 8192], P('section', None, 'expert'), may hold values from -0.0625 to 0.0625
- down_weight: bfloat16 [4, 8192, 7168], P('section', 'expert'), may hold values from -0.125 to 0.125
- query_nope: bfloat16 [4, 256, 2048], P('section', None, 'expert'), may hold values from -6 to 6
- query_rope: bfloat16 [4, 256, 1024], P('section', None, 'expert'), may hold values from -6 to 6
- key_nope: bfloat16 [4, 256, 2048], P('section', None, 'expert'), may hold values from -6 to 6
- key_rope: bfloat16 [4, 256, 64], P('section'), may hold values from -6 to 6
- value_heads: bfloat16 [4, 256, 2048], P('section', None, 'expert'), may hold values from -6 to 6
- upstream: bfloat16 [4, 256, 2048], P('section', None, 'expert'), may hold values from -24 to 24
Outputs:
- expert_mix: bfloat16 [4, 128, 7168], P('section', 'expert')
- query_grad: bfloat16 [4, 256, 2048], P('section', None, 'expert')
- rotary_grad: bfloat16 [4, 256, 1024], P('section', None, 'expert')
- key_grad: bfloat16 [4, 256, 2048], P('section', None, 'expert')
- value_grad: bfloat16 [4, 256, 2048], P('section', None, 'expert')
- shared_grad: float32 [4, 256, 64], P('section', 'expert')
The draws below stay inside these ranges and needn't reach their ends.
Inputs may be any that keep to these rules, and one draw needn't show every extreme that they name: `route_experts`: each token names 2 different experts. The 16 tokens of one device name each expert at most 16 times, and in every section one expert is named by every token of every device. `route_slots`: for each device and expert, the choices that name the expert have distinct slots.
All inputs are finite; a program needn't handle non-finite values.
Results may differ from the reference program's by a relative error of at most 0.008.
Values may be sent and summed in bfloat16 or wider, within the bound.
No kernel may reach another device: no remote copies, remote signals or barrier semaphores. Data moves between devices by JAX's collectives and lax.ppermute only.
A program may use at most 128 MiB of HBM per device.

```python
import math
import jax
import jax.numpy as jnp
from jax import lax

D = 7168
FF = 2048
EXPERTS = 4
TOP = 2
TOK_DEV = 16
SEQ = 256
NOPE = 128
ROPE = 64
VDIM = 128
SECTIONS = 4
TOKENS = 128
CAP = 16
HEADS = 16
N_EXPERT = 8


def routing_tables(key):
    base_key = jax.random.fold_in(key, 101)
    load_key, label_key, slot_key, order_key = jax.random.split(base_key, 4)
    sources = TOKENS // TOK_DEV
    others = EXPERTS - 1
    spread_total = (TOP - 1) * TOK_DEV
    base_load = spread_total // others
    leftover = spread_total - base_load * others
    wobble = max(min(CAP - base_load - 1, base_load - 1), 0)
    shifts = jax.random.randint(load_key, (SECTIONS, sources, others), 0, wobble + 1)
    extra_one = (jnp.arange(others) < leftover).astype(jnp.int32)
    rest_loads = base_load + extra_one[None, None, :] + shifts - jnp.roll(shifts, -1, axis=2)
    loads = jnp.concatenate([jnp.full((SECTIONS, sources, 1), CAP, jnp.int32), rest_loads.astype(jnp.int32)], axis=2)
    ends = jnp.cumsum(loads, axis=2)
    starts = ends - loads
    places = jnp.arange(TOP * TOK_DEV, dtype=jnp.int32)
    labels = jnp.sum((places[None, None, :, None] >= ends[:, :, None, :]).astype(jnp.int32), axis=3)
    local_slot = places[None, None, :] - jnp.take_along_axis(starts, labels, axis=2)
    relabel = jax.vmap(lambda one_key: jax.random.permutation(one_key, EXPERTS))(jax.random.split(label_key, SECTIONS))
    relabel = jnp.broadcast_to(relabel[:, None, :], (SECTIONS, sources, EXPERTS)).astype(jnp.int32)
    expert_seq = jnp.take_along_axis(relabel, labels, axis=2)
    slot_perms = jax.vmap(lambda one_key: jax.random.permutation(one_key, CAP))(jax.random.split(slot_key, SECTIONS * sources * EXPERTS))
    slot_perms = slot_perms.reshape(SECTIONS, sources, EXPERTS * CAP).astype(jnp.int32)
    slot_seq = jnp.take_along_axis(slot_perms, labels * CAP + local_slot, axis=2)
    token_order = jax.vmap(lambda one_key: jax.random.permutation(one_key, TOK_DEV))(jax.random.split(order_key, SECTIONS * sources))
    token_order = token_order.reshape(SECTIONS, sources, TOK_DEV).astype(jnp.int32)
    positions = token_order[:, :, :, None] + TOK_DEV * jnp.arange(TOP, dtype=jnp.int32)[None, None, None, :]
    positions = positions.reshape(SECTIONS, sources, TOK_DEV * TOP)
    chosen = jnp.take_along_axis(expert_seq, positions, axis=2).reshape(SECTIONS, TOKENS, TOP)
    slotted = jnp.take_along_axis(slot_seq, positions, axis=2).reshape(SECTIONS, TOKENS, TOP)
    return (chosen.astype(jnp.int32), slotted.astype(jnp.int32))


def draw_route_experts(key, part):
    return routing_tables(key)[0]


def draw_route_slots(key, part):
    return routing_tables(key)[1]


def query_key_fields(key):
    base_key = jax.random.fold_in(key, 202)
    query_key, key_key = jax.random.split(base_key, 2)
    field_shape = (SECTIONS, SEQ, HEADS * NOPE)
    queries = jax.random.truncated_normal(query_key, -4.0, 4.0, field_shape, jnp.float32)
    key_field = jax.random.truncated_normal(key_key, -4.0, 4.0, field_shape, jnp.float32)
    return (queries, key_field)


def draw_query_nope(key, part):
    return query_key_fields(key)[0].astype(jnp.bfloat16)


def draw_key_nope(key, part):
    return query_key_fields(key)[1].astype(jnp.bfloat16)


def steps_of(rng, shape, cuts, low, largest):
    factor_of, own = 1.0, jax.random.fold_in(rng, 6)
    for axis_at, shards_of in cuts:
        draws = jnp.exp(jax.random.uniform(jax.random.fold_in(own, axis_at), (shards_of,), jnp.float32, low / len(cuts), largest / len(cuts)))
        factor_of = factor_of * jnp.repeat(draws, shape[axis_at] // shards_of).reshape([-1 if axis == axis_at else 1 for axis in range(len(shape))])
    return factor_of


def centred(key, extent, deviation, most, cuts=(), kind=jnp.bfloat16):
    entries = deviation * jax.random.normal(key, extent, jnp.float32)
    if cuts:
        entries = entries * steps_of(key, extent, cuts, -0.22, 0.18)
    return jnp.clip(entries, -most, most).astype(kind)


def setup_inputs(seed: int = 0) -> dict:
    seeds = jax.random.split(jax.random.key(seed), 14)
    return {
        "tokens": centred(seeds[0], (SECTIONS, TOKENS, D), 1.0, 6.0, ((0, 4), (1, 8))),
        "route_experts": draw_route_experts(jax.random.fold_in(seeds[13], 71), 0),
        "route_slots": draw_route_slots(jax.random.fold_in(seeds[13], 71), 0),
        "route_weights": jnp.clip(0.1 + 0.9 * jax.random.uniform(seeds[3], (SECTIONS, TOKENS, TOP), jnp.float32) ** steps_of(seeds[3], (SECTIONS, TOKENS, TOP), ((0, 4), (1, 8)), -0.2, 0.2), 0.1, 1.0),
        "gate_weight": centred(seeds[4], (SECTIONS, D, EXPERTS * FF), D ** -0.5, 0.0625, ((0, 4), (2, 8))),
        "up_weight": centred(seeds[5], (SECTIONS, D, EXPERTS * FF), D ** -0.5, 0.0625, ((0, 4), (2, 8))),
        "down_weight": centred(seeds[6], (SECTIONS, EXPERTS * FF, D), FF ** -0.5, 0.125, ((0, 4), (1, 8))),
        "query_nope": draw_query_nope(jax.random.fold_in(seeds[13], 71), 0),
        "query_rope": centred(seeds[8], (SECTIONS, SEQ, HEADS * ROPE), 1.0, 6.0, ((0, 4), (2, 8))),
        "key_nope": draw_key_nope(jax.random.fold_in(seeds[13], 71), 0),
        "key_rope": centred(seeds[10], (SECTIONS, SEQ, ROPE), 1.0, 6.0, ((0, 4),)),
        "value_heads": centred(seeds[11], (SECTIONS, SEQ, HEADS * VDIM), 1.0, 6.0, ((0, 4), (2, 8))),
        "upstream": centred(seeds[12], (SECTIONS, SEQ, HEADS * VDIM), 4.0, 24.0, ((0, 4), (2, 8))),
    }


yarn_factor = 40.0
yarn_base = 10000.0
yarn_initial = 4096.0
yarn_fast = 32.0
yarn_slow = 1.0
mask_fill = -1.0e30


def correction_point(rotations, rope_width):
    return rope_width * math.log(yarn_initial / (rotations * 2.0 * math.pi)) / (2.0 * math.log(yarn_base))


def rotary_tables(length, rope_width):
    half_width = rope_width // 2
    lowest = max(math.floor(correction_point(yarn_fast, rope_width)), 0)
    highest = min(math.ceil(correction_point(yarn_slow, rope_width)), rope_width - 1)
    spread = max(highest - lowest, 0.001)
    unit_index = jnp.arange(half_width).astype(jnp.float32)
    extrapolated = 1.0 / (yarn_base ** (2.0 * unit_index / rope_width))
    interpolated = extrapolated / yarn_factor
    ramp_value = jnp.clip((unit_index - lowest) / spread, 0.0, 1.0)
    frequency = interpolated * ramp_value + extrapolated * (1.0 - ramp_value)
    angles = jnp.arange(length).astype(jnp.float32)[:, None] * frequency[None, :]
    return jnp.cos(angles), jnp.sin(angles)


def score_scale():
    magnitude = 0.1 * math.log(yarn_factor) + 1.0
    return (NOPE + ROPE) ** -0.5 * magnitude * magnitude


def rotate(operand, cosine_table, sine_table):
    paired = operand.reshape(operand.shape[:-1] + (operand.shape[-1] // 2, 2))
    first_part = paired[..., 0]
    second = paired[..., 1]
    turned = jnp.stack([first_part * cosine_table - second * sine_table,
                        first_part * sine_table + second * cosine_table], axis=-1)
    return turned.reshape(operand.shape)


def expert_section(tokens, route_experts, route_slots, route_weights, gate_weight, up_weight, down_weight):
    sources = TOKENS // TOK_DEV
    slice_count = N_EXPERT // EXPERTS
    slice_width = FF // slice_count
    source_of = jnp.broadcast_to((jnp.arange(TOKENS) // TOK_DEV).astype(jnp.int32)[:, None], (TOKENS, TOP))
    updates = jnp.broadcast_to(tokens[:, None, :], (TOKENS, TOP, D))
    dispatched = jnp.zeros((EXPERTS, sources, CAP, D), jnp.bfloat16)
    dispatched = dispatched.at[route_experts, source_of, route_slots].set(updates)
    gate_split = jnp.transpose(gate_weight.reshape(D, EXPERTS, FF), (1, 0, 2))
    up_split = jnp.transpose(up_weight.reshape(D, EXPERTS, FF), (1, 0, 2))
    down_split = down_weight.reshape(EXPERTS, FF, D)

    def one_expert(stacked):
        rows_in, gate_part, up_part, down_part = stacked
        flat_rows = rows_in.reshape(sources * CAP, D)
        gate_value = jnp.dot(flat_rows, gate_part, preferred_element_type=jnp.float32)
        up_value = jnp.dot(flat_rows, up_part, preferred_element_type=jnp.float32)
        hidden = (jax.nn.silu(gate_value) * up_value).astype(jnp.bfloat16)
        pieces = jnp.einsum("rgk,gkd->grd",
                            hidden.reshape(sources * CAP, slice_count, slice_width).astype(jnp.float32),
                            down_part.reshape(slice_count, slice_width, D).astype(jnp.float32))
        rounded = lax.optimization_barrier(pieces.astype(jnp.bfloat16))
        summed = jnp.sum(rounded.astype(jnp.float32), axis=0)
        return summed.astype(jnp.bfloat16).reshape(sources, CAP, D)

    expert_out = lax.map(one_expert, (dispatched, gate_split, up_split, down_split))
    expert_out = lax.optimization_barrier(expert_out)
    picked = expert_out[route_experts, source_of, route_slots]
    mixed = jnp.sum(picked.astype(jnp.float32) * route_weights[:, :, None], axis=1)
    return mixed.astype(jnp.bfloat16)


def head_grads(query_plain, query_turned, key_plain, key_turned, value_part, upstream_part, scale_value):
    length = query_plain.shape[0]
    scores = (jnp.dot(query_plain, key_plain.T, preferred_element_type=jnp.float32)
              + jnp.dot(query_turned, key_turned.T, preferred_element_type=jnp.float32)) * scale_value
    row_pos = jnp.arange(length)[:, None]
    col_pos = jnp.arange(length)[None, :]
    scores = jnp.where(col_pos <= row_pos, scores, mask_fill)
    row_top = jnp.max(scores, axis=1, keepdims=True)
    weights = jnp.exp(scores - row_top)
    softmaxed = weights / jnp.sum(weights, axis=1, keepdims=True)
    soft_low = softmaxed.astype(jnp.bfloat16)
    value_here = jnp.dot(soft_low.T, upstream_part, preferred_element_type=jnp.float32).astype(jnp.bfloat16)
    prob_grad = jnp.dot(upstream_part, value_part.T, preferred_element_type=jnp.float32)
    row_sum = jnp.sum(softmaxed * prob_grad, axis=1, keepdims=True)
    score_grad = (scale_value * softmaxed * (prob_grad - row_sum)).astype(jnp.bfloat16)
    query_here = jnp.dot(score_grad, key_plain, preferred_element_type=jnp.float32).astype(jnp.bfloat16)
    turned_query = jnp.dot(score_grad, key_turned, preferred_element_type=jnp.float32)
    key_here = jnp.dot(score_grad.T, query_plain, preferred_element_type=jnp.float32).astype(jnp.bfloat16)
    turned_key = jnp.dot(score_grad.T, query_turned, preferred_element_type=jnp.float32)
    return query_here, turned_query, key_here, value_here, turned_key


def attention_section(query_nope, query_rope, key_nope, key_rope, value_heads, upstream):
    cosine_table, sine_table = rotary_tables(SEQ, ROPE)
    scale_value = score_scale()
    query_plain = query_nope.reshape(SEQ, HEADS, NOPE)
    query_turned = rotate(query_rope.reshape(SEQ, HEADS, ROPE).astype(jnp.float32),
                          cosine_table[:, None, :], sine_table[:, None, :]).astype(jnp.bfloat16)
    key_turned = rotate(key_rope.astype(jnp.float32), cosine_table, sine_table).astype(jnp.bfloat16)
    key_plain = key_nope.reshape(SEQ, HEADS, NOPE)
    value_split = value_heads.reshape(SEQ, HEADS, VDIM)
    upstream_split = upstream.reshape(SEQ, HEADS, VDIM)

    def one_head(stacked):
        return head_grads(stacked[0], stacked[1], stacked[2], key_turned, stacked[3], stacked[4], scale_value)

    per_head = lax.map(one_head, (jnp.moveaxis(query_plain, 1, 0), jnp.moveaxis(query_turned, 1, 0),
                                  jnp.moveaxis(key_plain, 1, 0), jnp.moveaxis(value_split, 1, 0),
                                  jnp.moveaxis(upstream_split, 1, 0)))
    query_here, turned_query, key_here, value_here, turned_key = per_head
    rotary_here = rotate(turned_query, cosine_table, -sine_table).astype(jnp.bfloat16)
    shared_here = rotate(jnp.sum(turned_key, axis=0), cosine_table, -sine_table)

    def heads_last(operand):
        return jnp.moveaxis(operand, 0, 1).reshape(SEQ, -1)

    return heads_last(query_here), heads_last(rotary_here), heads_last(key_here), heads_last(value_here), shared_here


def to_previous(operand):
    return jnp.concatenate([operand[1:], jnp.zeros_like(operand[:1])], axis=0)


def reference(tokens, route_experts, route_slots, route_weights, gate_weight, up_weight, down_weight,
              query_nope, query_rope, key_nope, key_rope, value_heads, upstream):
    def expert_step(stacked):
        return expert_section(stacked[0], stacked[1], stacked[2], stacked[3], stacked[4], stacked[5], stacked[6])

    expert_mix = lax.map(expert_step, (tokens, route_experts, route_slots, route_weights,
                                       gate_weight, up_weight, down_weight))

    def attention_step(stacked):
        return attention_section(stacked[0], stacked[1], stacked[2], stacked[3], stacked[4], stacked[5])

    section_grads = lax.map(attention_step, (query_nope, query_rope, key_nope, key_rope, value_heads, upstream))
    query_grad = to_previous(section_grads[0])
    rotary_grad = to_previous(section_grads[1])
    key_grad = to_previous(section_grads[2])
    value_grad = to_previous(section_grads[3])
    shared_grad = to_previous(section_grads[4])
    return (expert_mix, query_grad, rotary_grad, key_grad, value_grad, shared_grad)
```

```python
import functools
import math

import jax
import jax.numpy as jnp
import numpy as np
from jax import lax
from jax.experimental import pallas as pl
from jax.experimental.pallas import tpu as pltpu
from jax.sharding import PartitionSpec as P

EXPERTS = 4
TOP = 2
NOPE = 128
ROPE = 64
VDIM = 128

yarn_factor = 40.0
yarn_base = 10000.0
yarn_initial = 4096.0
yarn_fast = 32.0
yarn_slow = 1.0
mask_fill = -1e30

IN_CHUNKS = 2
OUT_CHUNKS = 2
VMEM = 32 * 1024 * 1024


def from_behind(array, axis, by):
    size = lax.axis_size(axis)
    pairs = [(i, i + by) for i in range(size) if 0 <= i + by < size]
    return lax.ppermute(array, axis, pairs)


def swap_xor(array, offset):
    size = lax.axis_size("expert")
    return lax.ppermute(array, "expert", [(i, i ^ offset) for i in range(size)])


def correction_point(rotations, rope_width):
    return (
        rope_width
        * math.log(yarn_initial / (rotations * 2.0 * math.pi))
        / (2.0 * math.log(yarn_base))
    )


def rotary_tables(length, rope_width):
    half_width = rope_width // 2
    lowest = max(math.floor(correction_point(yarn_fast, rope_width)), 0)
    highest = min(math.ceil(correction_point(yarn_slow, rope_width)), rope_width - 1)
    spread = np.float32(max(highest - lowest, 0.001))
    unit_index = np.arange(half_width).astype(np.float32)
    extrapolated = np.float32(1.0) / np.power(
        np.float32(yarn_base), np.float32(2.0) * unit_index / np.float32(rope_width)
    ).astype(np.float32)
    interpolated = extrapolated / np.float32(yarn_factor)
    ramp_value = np.clip((unit_index - np.float32(lowest)) / spread, 0.0, 1.0).astype(np.float32)
    frequency = interpolated * ramp_value + extrapolated * (np.float32(1.0) - ramp_value)
    angles = np.arange(length).astype(np.float32)[:, None] * frequency[None, :]
    cosine = np.cos(angles.astype(np.float64)).astype(np.float32)
    sine = np.sin(angles.astype(np.float64)).astype(np.float32)
    cosine = np.repeat(cosine, 2, axis=1)
    sine = np.repeat(sine, 2, axis=1) * np.tile(np.array([-1.0, 1.0], np.float32), half_width)
    return np.tile(cosine, (1, 2)), np.tile(sine, (1, 2))


def score_scale():
    magnitude = 0.1 * math.log(yarn_factor) + 1.0
    return (NOPE + ROPE) ** (-0.5) * magnitude * magnitude


def dot(left, right, left_dim, right_dim):
    return lax.dot_general(
        left, right, (((left_dim,), (right_dim,)), ((), ())), preferred_element_type=jnp.float32
    )


def swap_pairs(value):
    lanes = value.shape[1]
    lane = lax.broadcasted_iota(jnp.int32, value.shape, 1)
    return jnp.where(lane % 2 == 0, pltpu.roll(value, lanes - 1, 1), pltpu.roll(value, 1, 1))


def attention_kernel(
    query_ref,
    rope_ref,
    key_ref,
    key_rope_ref,
    value_ref,
    upstream_ref,
    cosine_ref,
    sine_ref,
    query_out,
    rotary_out,
    key_out,
    value_out,
    shared_out,
):
    length = query_ref.shape[0]
    head_count = query_ref.shape[1] // NOPE
    scale_value = score_scale()
    cosine = cosine_ref[...]
    sine = sine_ref[...]
    key_pair = key_rope_ref[...].astype(jnp.float32)
    key_pair = jnp.concatenate([key_pair, key_pair], axis=1)
    key_turned = (key_pair * cosine + swap_pairs(key_pair) * sine).astype(jnp.bfloat16)
    row_pos = lax.broadcasted_iota(jnp.int32, (length, length), 0)
    col_pos = lax.broadcasted_iota(jnp.int32, (length, length), 1)
    seen = col_pos <= row_pos
    low_half = lax.broadcasted_iota(jnp.int32, (length, 2 * ROPE), 1) < ROPE
    shared = jnp.zeros((length, 2 * ROPE), jnp.float32)
    for pair in range(head_count // 2):
        both = slice(pair * 2 * ROPE, (pair + 1) * 2 * ROPE)
        rope = rope_ref[:, both].astype(jnp.float32)
        turned = rope * cosine + swap_pairs(rope) * sine
        rotary = jnp.zeros((length, 2 * ROPE), jnp.float32)
        for side in range(2):
            own = low_half if side == 0 else jnp.logical_not(low_half)
            head = slice((pair * 2 + side) * NOPE, (pair * 2 + side + 1) * NOPE)
            mine = jnp.where(own, turned, 0.0).astype(jnp.bfloat16)
            query = jnp.concatenate([query_ref[:, head], mine], axis=1)
            key = jnp.concatenate([key_ref[:, head], key_turned], axis=1)
            upstream = upstream_ref[:, head]
            scores = dot(query, key, 1, 1) * scale_value
            scores = jnp.where(seen, scores, mask_fill)
            row_top = jnp.max(scores, axis=1, keepdims=True)
            weights = jnp.exp(scores - row_top)
            softmaxed = weights / jnp.sum(weights, axis=1, keepdims=True)
            value_out[:, head] = dot(softmaxed.astype(jnp.bfloat16), upstream, 0, 0).astype(
                jnp.bfloat16
            )
            prob_grad = dot(upstream, value_ref[:, head], 1, 1)
            row_sum = jnp.sum(softmaxed * prob_grad, axis=1, keepdims=True)
            score_grad = (scale_value * softmaxed * (prob_grad - row_sum)).astype(jnp.bfloat16)
            by_query = dot(score_grad, key, 1, 0)
            by_key = dot(score_grad, query, 0, 0)
            query_out[:, head] = by_query[:, :NOPE].astype(jnp.bfloat16)
            key_out[:, head] = by_key[:, :NOPE].astype(jnp.bfloat16)
            rotary = jnp.where(own, by_query[:, NOPE:], rotary)
            shared = shared + by_key[:, NOPE:]
        rotary_out[:, both] = (rotary * cosine - swap_pairs(rotary) * sine).astype(jnp.bfloat16)
    shared = shared + pltpu.roll(shared, ROPE, 1)
    shared_out[...] = (shared * cosine - swap_pairs(shared) * sine)[:, :ROPE]


def attention_grads(query_nope, query_rope, key_nope, key_rope, value_heads, upstream):
    length = query_nope.shape[0]
    cosine, sine = rotary_tables(length, ROPE)
    like = jax.ShapeDtypeStruct
    return pl.pallas_call(
        attention_kernel,
        out_shape=(
            like(query_nope.shape, jnp.bfloat16),
            like(query_rope.shape, jnp.bfloat16),
            like(key_nope.shape, jnp.bfloat16),
            like(value_heads.shape, jnp.bfloat16),
            like(key_rope.shape, jnp.float32),
        ),
        compiler_params=pltpu.CompilerParams(vmem_limit_bytes=VMEM),
        cost_estimate=pl.CostEstimate(
            flops=4_000_000_000, bytes_accessed=2_000_000, transcendentals=200_000
        ),
        name="attention_grads",
    )(
        query_nope,
        query_rope,
        key_nope,
        key_rope,
        value_heads,
        upstream,
        jnp.asarray(cosine),
        jnp.asarray(sine),
    )


def tile_of(extent, most):
    return max(t for t in range(128, most + 1, 128) if extent % t == 0)


def projection_kernel(count, first, last, *refs):
    blocks = refs[:count]
    gate_ref, up_ref = refs[count : count + 2]
    rest = refs[count + 2 :]
    step = pl.program_id(0)
    if first:
        before = None
    else:
        before, rest = rest[:2], rest[2:]
    if last:
        hidden_ref, gate_sum, up_sum = rest
    else:
        gate_sum, up_sum = rest
    rows = jnp.concatenate([b[...] for b in blocks], axis=0)
    gate = jnp.dot(rows, gate_ref[...], preferred_element_type=jnp.float32)
    up = jnp.dot(rows, up_ref[...], preferred_element_type=jnp.float32)

    @pl.when(step == 0)
    def _():
        gate_sum[...] = gate if first else gate + before[0][...]
        up_sum[...] = up if first else up + before[1][...]

    @pl.when(step > 0)
    def _():
        gate_sum[...] += gate
        up_sum[...] += up

    if last:

        @pl.when(step == pl.num_programs(0) - 1)
        def _():
            value = gate_sum[...]
            hidden_ref[...] = (value / (1.0 + jnp.exp(-value)) * up_sum[...]).astype(jnp.bfloat16)


def projections(blocks, gate_part, up_part, at, before, last):
    count = len(blocks)
    block_rows, width = blocks[0].shape
    rows, hidden_width = count * block_rows, gate_part.shape[1]
    tile = tile_of(width, 896)
    begin = at // tile
    whole = pl.BlockSpec((rows, hidden_width), lambda k: (0, 0))
    weight = pl.BlockSpec((tile, hidden_width), lambda k: (begin + k, 0))
    total = jax.ShapeDtypeStruct((rows, hidden_width), jnp.float32)
    first = before is None
    return pl.pallas_call(
        functools.partial(projection_kernel, count, first, last),
        grid=(width // tile,),
        in_specs=[pl.BlockSpec((block_rows, tile), lambda k: (0, k))] * count
        + [weight, weight]
        + ([] if first else [whole, whole]),
        out_specs=whole if last else (whole, whole),
        out_shape=jax.ShapeDtypeStruct((rows, hidden_width), jnp.bfloat16)
        if last
        else (total, total),
        scratch_shapes=[pltpu.VMEM((rows, hidden_width), jnp.float32)] * 2 if last else [],
        compiler_params=pltpu.CompilerParams(vmem_limit_bytes=VMEM),
        cost_estimate=pl.CostEstimate(
            flops=4 * rows * width * hidden_width,
            bytes_accessed=4 * width * hidden_width + 2 * rows * width,
            transcendentals=0,
        ),
        name="gate_and_up",
    )(*blocks, gate_part, up_part, *([] if first else before))


def down_kernel(hidden_ref, down_ref, keep_ref, send_ref):
    out = jnp.dot(hidden_ref[...], down_ref[...], preferred_element_type=jnp.float32)
    half = keep_ref.shape[0]
    keep_ref[...] = out[:half].astype(jnp.bfloat16)
    send_ref[...] = out[half:].astype(jnp.bfloat16)


def down_columns(hidden, down_part, at, width):
    rows, depth = hidden.shape
    tile = tile_of(width, 1024)
    begin = at // tile
    half = pl.BlockSpec((rows // 2, tile), lambda j: (0, j))
    out = jax.ShapeDtypeStruct((rows // 2, width), jnp.bfloat16)
    return pl.pallas_call(
        down_kernel,
        grid=(width // tile,),
        in_specs=[
            pl.BlockSpec((rows, depth), lambda j: (0, 0)),
            pl.BlockSpec((depth, tile), lambda j: (0, begin + j)),
        ],
        out_specs=(half, half),
        out_shape=(out, out),
        compiler_params=pltpu.CompilerParams(vmem_limit_bytes=VMEM),
        cost_estimate=pl.CostEstimate(
            flops=2 * rows * depth * width,
            bytes_accessed=2 * depth * width + 2 * rows * width,
            transcendentals=0,
        ),
        name="down",
    )(hidden, down_part)


def add_kernel(parts, kept_ref, came_ref, *outs):
    total = (kept_ref[...].astype(jnp.float32) + came_ref[...].astype(jnp.float32)).astype(
        jnp.bfloat16
    )
    rows = total.shape[0] // parts
    for i in range(parts):
        outs[i][...] = total[i * rows : (i + 1) * rows]


def add_parts(kept, came, parts):
    rows, width = kept.shape
    out = jax.ShapeDtypeStruct((rows // parts, width), jnp.bfloat16)
    return pl.pallas_call(
        functools.partial(add_kernel, parts),
        out_shape=(out,) * parts,
        compiler_params=pltpu.CompilerParams(vmem_limit_bytes=VMEM),
        cost_estimate=pl.CostEstimate(
            flops=rows * width, bytes_accessed=6 * rows * width, transcendentals=0
        ),
        name="add_slices",
    )(kept, came)


def mix_kernel(chunks, weights_ref, *refs):
    out_ref = refs[-1]
    at = 0
    for c in range(chunks):
        group = refs[c * EXPERTS : (c + 1) * EXPERTS]
        width = group[0].shape[1]
        total = weights_ref[:, 0:1] * group[0][...].astype(jnp.float32)
        for k in range(1, EXPERTS):
            total = total + weights_ref[:, k : k + 1] * group[k][...].astype(jnp.float32)
        out_ref[:, at : at + width] = total.astype(jnp.bfloat16)
        at += width


def mix(weights, blocks):
    rows = weights.shape[0]
    width = sum(b[0].shape[1] for b in blocks)
    flat = [b for group in blocks for b in group]
    return pl.pallas_call(
        functools.partial(mix_kernel, len(blocks)),
        out_shape=jax.ShapeDtypeStruct((rows, width), jnp.bfloat16),
        compiler_params=pltpu.CompilerParams(vmem_limit_bytes=VMEM),
        cost_estimate=pl.CostEstimate(
            flops=8 * rows * width, bytes_accessed=10 * rows * width, transcendentals=0
        ),
        name="mix",
    )(weights, *flat)


def gathered(rows, group):
    blocks = {0: rows}
    for k in range(1, EXPERTS):
        blocks[k * group] = swap_xor(rows, k * group)
    bit = 1
    while bit < group:
        for j in sorted(blocks):
            blocks[j + bit] = swap_xor(blocks[j], bit)
        bit *= 2
    return blocks


def order_of(group):
    order = [k * group for k in range(EXPERTS)]
    bit = 1
    while bit < group:
        order = order + [j + bit for j in order]
        bit *= 2
    return order


def mixture(tokens, route_experts, route_slots, route_weights, gate_part, up_part, down_part):
    model_width = tokens.shape[1]
    group = lax.axis_size("expert") // EXPERTS
    order = order_of(group)
    step = model_width // IN_CHUNKS
    sums = None
    for c in range(IN_CHUNKS):
        blocks = gathered(tokens[:, c * step : (c + 1) * step], group)
        sums = projections(
            [blocks[j] for j in order], gate_part, up_part, c * step, sums, c == IN_CHUNKS - 1
        )
    hidden = sums
    step = model_width // OUT_CHUNKS
    mixed = []
    for c in range(OUT_CHUNKS):
        kept, sent = down_columns(hidden, down_part, c * step, step)
        bit = group // 2
        while bit > 1:
            kept = kept.astype(jnp.float32) + swap_xor(sent, bit).astype(jnp.float32)
            kept = kept.astype(jnp.bfloat16)
            kept, sent = jnp.split(kept, 2)
            bit //= 2
        parts = add_parts(kept, swap_xor(sent, 1), EXPERTS)
        mixed.append(
            [parts[0]] + [swap_xor(parts[k], k * group) for k in range(1, EXPERTS)]
        )
    mine = lax.axis_index("expert") // group
    chosen = jnp.bitwise_xor(mine, jnp.arange(EXPERTS, dtype=jnp.int32))
    weights = jnp.sum(
        jnp.where(route_experts[:, :, None] == chosen, route_weights[:, :, None], 0.0), axis=1
    )
    return mix(weights, mixed)


def per_device(
    tokens,
    route_experts,
    route_slots,
    route_weights,
    gate_weight,
    up_weight,
    down_weight,
    query_nope,
    query_rope,
    key_nope,
    key_rope,
    value_heads,
    upstream,
):
    query_here, rotary_here, key_here, value_here, shared_turn = attention_grads(
        query_nope[0], query_rope[0], key_nope[0], key_rope[0], value_heads[0], upstream[0]
    )
    shared_local = lax.psum_scatter(shared_turn, "expert", scatter_dimension=0, tiled=True)
    moved = from_behind((query_here, rotary_here, key_here, value_here), "section", -1)
    shared_grad = from_behind(shared_local, "section", -1)
    expert_mix = mixture(
        tokens[0],
        route_experts[0],
        route_slots[0],
        route_weights[0],
        gate_weight[0],
        up_weight[0],
        down_weight[0],
    )
    return (
        expert_mix[None],
        moved[0][None],
        moved[1][None],
        moved[2][None],
        moved[3][None],
        shared_grad[None],
    )


def solution(mesh):
    return jax.shard_map(
        per_device,
        mesh=mesh,
        in_specs=(
            P("section", "expert", None),
            P("section", "expert", None),
            P("section", "expert", None),
            P("section", "expert", None),
            P("section", None, "expert"),
            P("section", None, "expert"),
            P("section", "expert", None),
            P("section", None, "expert"),
            P("section", None, "expert"),
            P("section", None, "expert"),
            P("section", None, None),
            P("section", None, "expert"),
            P("section", None, "expert"),
        ),
        out_specs=(
            P("section", "expert", None),
            P("section", None, "expert"),
            P("section", None, "expert"),
            P("section", None, "expert"),
            P("section", None, "expert"),
            P("section", "expert", None),
        ),
        check_vma=False,
    )
```

```python
import functools
import math

import jax
import jax.numpy as jnp
import numpy as np
from jax import lax
from jax.experimental import pallas as pl
from jax.experimental.pallas import tpu as pltpu
from jax.sharding import PartitionSpec as P

EXPERTS = 4
TOP = 2
NOPE = 128
ROPE = 64
VDIM = 128

yarn_factor = 40.0
yarn_base = 10000.0
yarn_initial = 4096.0
yarn_fast = 32.0
yarn_slow = 1.0
mask_fill = -1e30

OUT_SPLIT = (1, 2)
TILE = 1024
LANES = 128
VMEM = 8 * 1024 * 1024
HEAD_VMEM = 8 * 1024 * 1024
HOLD_VMEM = 11 * 1024 * 1024


def in_hbm(array):
    return pltpu.with_memory_space_constraint(array, pltpu.HBM)


def in_vmem(array):
    return pltpu.with_memory_space_constraint(array, pltpu.VMEM)


def from_behind(array, axis, by):
    size = lax.axis_size(axis)
    pairs = [(i, i + by) for i in range(size) if 0 <= i + by < size]
    return lax.ppermute(array, axis, pairs)


def swap_xor(array, offset):
    size = lax.axis_size("expert")
    return lax.ppermute(array, "expert", [(i, i ^ offset) for i in range(size)])


def correction_point(rotations, rope_width):
    return (
        rope_width
        * math.log(yarn_initial / (rotations * 2.0 * math.pi))
        / (2.0 * math.log(yarn_base))
    )


def rotary_tables(length, rope_width):
    half_width = rope_width // 2
    lowest = max(math.floor(correction_point(yarn_fast, rope_width)), 0)
    highest = min(math.ceil(correction_point(yarn_slow, rope_width)), rope_width - 1)
    spread = np.float32(max(highest - lowest, 0.001))
    unit_index = np.arange(half_width).astype(np.float32)
    extrapolated = np.float32(1.0) / np.power(
        np.float32(yarn_base), np.float32(2.0) * unit_index / np.float32(rope_width)
    ).astype(np.float32)
    interpolated = extrapolated / np.float32(yarn_factor)
    ramp_value = np.clip((unit_index - np.float32(lowest)) / spread, 0.0, 1.0).astype(np.float32)
    frequency = interpolated * ramp_value + extrapolated * (np.float32(1.0) - ramp_value)
    angles = np.arange(length).astype(np.float32)[:, None] * frequency[None, :]
    cosine = np.cos(angles.astype(np.float64)).astype(np.float32)
    sine = np.sin(angles.astype(np.float64)).astype(np.float32)
    cosine = np.repeat(cosine, 2, axis=1)
    sine = np.repeat(sine, 2, axis=1) * np.tile(np.array([-1.0, 1.0], np.float32), half_width)
    return np.tile(cosine, (1, 2)), np.tile(sine, (1, 2))


def score_scale():
    magnitude = 0.1 * math.log(yarn_factor) + 1.0
    return (NOPE + ROPE) ** (-0.5) * magnitude * magnitude


def dot(left, right, left_dim, right_dim):
    return lax.dot_general(
        left, right, (((left_dim,), (right_dim,)), ((), ())), preferred_element_type=jnp.float32
    )


def fold_of(per_dest, block_rows):
    folds = max(per_dest // block_rows, 1)
    return folds, per_dest // folds


def swap_pairs(value):
    lanes = value.shape[1]
    lane = lax.broadcasted_iota(jnp.int32, value.shape, 1)
    return jnp.where(lane % 2 == 0, pltpu.roll(value, lanes - 1, 1), pltpu.roll(value, 1, 1))


def split_moving(ref, nope, values, rope):
    widths = (nope, nope, values, rope)
    views, at = [], 0
    for width in widths:
        views.append(ref.at[:, at : at + width])
        at += width
    return views


def attention_kernel(
    query_ref,
    rope_ref,
    key_ref,
    key_rope_ref,
    value_ref,
    upstream_ref,
    cosine_ref,
    sine_ref,
    me_ref,
    down_ref,
    moving_out,
    extra_out,
    down_out,
    shared_scratch,
    down_sem,
    *,
    order,
    block_rows,
):
    fetch = pltpu.make_async_copy(down_ref.at[:, : down_out.shape[1]], down_out, down_sem)
    fetch.start()
    length = query_ref.shape[0]
    head_count = query_ref.shape[1] // NOPE
    query_out, key_out, value_out, rotary_out = split_moving(
        moving_out, query_ref.shape[1], value_ref.shape[1], rope_ref.shape[1]
    )
    scale_value = score_scale()
    cosine = cosine_ref[...]
    sine = sine_ref[...]
    key_pair = key_rope_ref[...].astype(jnp.float32)
    key_pair = jnp.concatenate([key_pair, key_pair], axis=1)
    key_turned = (key_pair * cosine + swap_pairs(key_pair) * sine).astype(jnp.bfloat16)
    row_pos = lax.broadcasted_iota(jnp.int32, (length, length), 0)
    col_pos = lax.broadcasted_iota(jnp.int32, (length, length), 1)
    seen = col_pos <= row_pos
    low_half = lax.broadcasted_iota(jnp.int32, (length, 2 * ROPE), 1) < ROPE
    shared = jnp.zeros((length, 2 * ROPE), jnp.float32)
    for pair in range(head_count // 2):
        both = slice(pair * 2 * ROPE, (pair + 1) * 2 * ROPE)
        rope = rope_ref[:, both].astype(jnp.float32)
        turned = rope * cosine + swap_pairs(rope) * sine
        rotary = jnp.zeros((length, 2 * ROPE), jnp.float32)
        for side in range(2):
            own = low_half if side == 0 else jnp.logical_not(low_half)
            head = slice((pair * 2 + side) * NOPE, (pair * 2 + side + 1) * NOPE)
            mine = jnp.where(own, turned, 0.0).astype(jnp.bfloat16)
            query = jnp.concatenate([query_ref[:, head], mine], axis=1)
            key = jnp.concatenate([key_ref[:, head], key_turned], axis=1)
            upstream = upstream_ref[:, head]
            scores = dot(query, key, 1, 1) * scale_value
            scores = jnp.where(seen, scores, mask_fill)
            row_top = jnp.max(scores, axis=1, keepdims=True)
            weights = jnp.exp(scores - row_top)
            softmaxed = weights / jnp.sum(weights, axis=1, keepdims=True)
            value_out[:, head] = dot(softmaxed.astype(jnp.bfloat16), upstream, 0, 0).astype(
                jnp.bfloat16
            )
            prob_grad = dot(upstream, value_ref[:, head], 1, 1)
            row_sum = jnp.sum(softmaxed * prob_grad, axis=1, keepdims=True)
            score_grad = (scale_value * softmaxed * (prob_grad - row_sum)).astype(jnp.bfloat16)
            by_query = dot(score_grad, key, 1, 0)
            by_key = dot(score_grad, query, 0, 0)
            query_out[:, head] = by_query[:, :NOPE].astype(jnp.bfloat16)
            key_out[:, head] = by_key[:, :NOPE].astype(jnp.bfloat16)
            rotary = jnp.where(own, by_query[:, NOPE:], rotary)
            shared = shared + by_key[:, NOPE:]
        rotary_out[:, both] = (rotary * cosine - swap_pairs(rotary) * sine).astype(jnp.bfloat16)
    shared = shared + pltpu.roll(shared, ROPE, 1)
    shared = shared * cosine - swap_pairs(shared) * sine
    high = shared.astype(jnp.bfloat16).astype(jnp.float32)
    shared_scratch[...] = jnp.where(low_half, high, shared - high)
    per_dest = length // len(order)
    folds, rows = fold_of(per_dest, block_rows)
    if rows < block_rows:
        extra_out[...] = jnp.zeros_like(extra_out)
    for place, index in enumerate(order):
        begin = (me_ref[0] ^ index) * per_dest
        for fold in range(folds):
            piece = shared_scratch[pl.ds(pl.multiple_of(begin + fold * rows, 8), rows), :]
            if rows < block_rows:
                piece = jnp.concatenate(
                    [piece, jnp.zeros((block_rows - rows, LANES), jnp.float32)], axis=0
                )
            extra_out[
                place * block_rows : (place + 1) * block_rows, fold * LANES : (fold + 1) * LANES
            ] = piece.astype(jnp.bfloat16)
    fetch.wait()


def attention_grads(
    query_nope, query_rope, key_nope, key_rope, value_heads, upstream, me, order, block_rows,
    down_part, down_width,
):
    length = query_nope.shape[0]
    cosine, sine = rotary_tables(length, ROPE)
    like = jax.ShapeDtypeStruct
    width = 2 * query_nope.shape[1] + value_heads.shape[1] + query_rope.shape[1]
    folds, _ = fold_of(length // len(order), block_rows)
    here = pl.BlockSpec(memory_space=pltpu.VMEM)
    return pl.pallas_call(
        functools.partial(attention_kernel, order=order, block_rows=block_rows),
        in_specs=[here] * 8
        + [pl.BlockSpec(memory_space=pltpu.SMEM), pl.BlockSpec(memory_space=pl.ANY)],
        out_specs=(here, here, here),
        scratch_shapes=[pltpu.VMEM((length, 2 * ROPE), jnp.float32), pltpu.SemaphoreType.DMA(())],
        out_shape=(
            like((length, width), jnp.bfloat16),
            like((len(order) * block_rows, folds * LANES), jnp.bfloat16),
            pltpu.VMEM((down_part.shape[0], down_width), down_part.dtype),
        ),
        compiler_params=pltpu.CompilerParams(vmem_limit_bytes=HEAD_VMEM),
        cost_estimate=pl.CostEstimate(
            flops=4_000_000_000, bytes_accessed=2_000_000, transcendentals=200_000
        ),
        name="attention_grads",
    )(
        in_hbm(query_nope),
        in_hbm(query_rope),
        in_hbm(key_nope),
        in_hbm(key_rope),
        in_hbm(value_heads),
        in_hbm(upstream),
        in_hbm(jnp.asarray(cosine)),
        in_hbm(jnp.asarray(sine)),
        me,
        in_hbm(down_part),
    )


def settle_kernel(moved_ref, after_ref, query_out, key_out, value_out, rotary_out):
    del after_ref
    views = split_moving(moved_ref, query_out.shape[1], value_out.shape[1], rotary_out.shape[1])
    for view, out in zip(views, (query_out, key_out, value_out, rotary_out)):
        out[...] = view[...]


def settle(moved, nope, values, rope, after):
    length = moved.shape[0]
    out = [jax.ShapeDtypeStruct((length, w), moved.dtype) for w in (nope, nope, values, rope)]
    return pl.pallas_call(
        settle_kernel,
        in_specs=[pl.BlockSpec(memory_space=pltpu.VMEM), pl.BlockSpec(memory_space=pl.ANY)],
        out_shape=tuple(out),
        compiler_params=pltpu.CompilerParams(vmem_limit_bytes=VMEM),
        cost_estimate=pl.CostEstimate(
            flops=0, bytes_accessed=4 * moved.size, transcendentals=0
        ),
        name="settle",
    )(moved, after)


def tile_of(extent, most):
    return max(t for t in range(128, most + 1, 128) if extent % t == 0)


def hold_kernel(gate_ref, up_ref, after_ref, gate_out, up_out, token_out, sems):
    del after_ref
    token_out[...] = jnp.zeros_like(token_out)
    copies = [
        pltpu.make_async_copy(gate_ref, gate_out, sems.at[0]),
        pltpu.make_async_copy(up_ref, up_out, sems.at[1]),
    ]
    for copy in copies:
        copy.start()
    for copy in copies:
        copy.wait()


def hold(gate_part, up_part, after):
    here = pl.BlockSpec(memory_space=pltpu.VMEM)
    return pl.pallas_call(
        hold_kernel,
        in_specs=[pl.BlockSpec(memory_space=pl.ANY)] * 3,
        out_specs=(here, here, here),
        out_shape=(
            pltpu.VMEM(gate_part.shape, gate_part.dtype),
            pltpu.VMEM(up_part.shape, up_part.dtype),
            jax.ShapeDtypeStruct((8, LANES), jnp.float32),
        ),
        scratch_shapes=[pltpu.SemaphoreType.DMA((2,))],
        compiler_params=pltpu.CompilerParams(vmem_limit_bytes=HOLD_VMEM),
        cost_estimate=pl.CostEstimate(
            flops=0, bytes_accessed=4 * gate_part.size, transcendentals=0
        ),
        name="hold",
    )(in_hbm(gate_part), in_hbm(up_part), after)


def experts_kernel(count, *refs):
    blocks = refs[:count]
    gate_ref, up_ref, held_ref, down_ref, extra_ref = refs[count : count + 5]
    kept_refs, sent_refs = refs[count + 6 : count + 8], refs[count + 8 : count + 10]
    gate_sum, up_sum, hidden_ref, rest_ref, sem = refs[count + 10 :]
    first = held_ref.shape[1]
    fetch = pltpu.make_async_copy(down_ref.at[:, first:], rest_ref, sem)
    fetch.start()
    width = blocks[0].shape[1]
    tile = tile_of(width, TILE)
    for i in range(width // tile):
        there = slice(i * tile, (i + 1) * tile)
        rows = jnp.concatenate([b[:, there] for b in blocks], axis=0)
        gate = jnp.dot(rows, gate_ref[there], preferred_element_type=jnp.float32)
        up = jnp.dot(rows, up_ref[there], preferred_element_type=jnp.float32)
        if i > 0:
            gate, up = gate_sum[...] + gate, up_sum[...] + up
        gate_sum[...] = gate
        up_sum[...] = up
    gate = gate_sum[...]
    hidden_ref[...] = (gate / (1.0 + jnp.exp(-gate)) * up_sum[...]).astype(jnp.bfloat16)
    half = hidden_ref.shape[0] // 2
    for part, (weights, kept, sent) in enumerate(
        zip((held_ref, rest_ref), kept_refs, sent_refs)
    ):
        if part == 1:
            fetch.wait()
        width = weights.shape[1]
        tile = tile_of(width, TILE)
        for i in range(width // tile):
            there = slice(i * tile, (i + 1) * tile)
            out = jnp.dot(hidden_ref[...], weights[:, there], preferred_element_type=jnp.float32)
            kept[:, there] = out[:half].astype(jnp.bfloat16)
            sent[:, there] = out[half:].astype(jnp.bfloat16)
        if part == 0:
            kept[:, width:] = extra_ref[:half]
            sent[:, width:] = extra_ref[half:]


def experts(blocks, gate_held, up_held, down_held, down_part, extra, after):
    count = len(blocks)
    block_rows, width = blocks[0].shape
    rows, hidden_width = count * block_rows, gate_held.shape[1]
    first = down_held.shape[1]
    rest = width - first
    here = pl.BlockSpec(memory_space=pltpu.VMEM)
    anywhere = pl.BlockSpec(memory_space=pl.ANY)
    out = [
        jax.ShapeDtypeStruct((rows // 2, w), jnp.bfloat16)
        for w in (first + extra.shape[1], rest)
    ]
    return pl.pallas_call(
        functools.partial(experts_kernel, count),
        in_specs=[here] * (count + 3) + [anywhere, here, anywhere],
        out_shape=(*out, *out),
        scratch_shapes=[
            pltpu.VMEM((rows, hidden_width), jnp.float32),
            pltpu.VMEM((rows, hidden_width), jnp.float32),
            pltpu.VMEM((rows, hidden_width), jnp.bfloat16),
            pltpu.VMEM((hidden_width, rest), jnp.bfloat16),
            pltpu.SemaphoreType.DMA(()),
        ],
        compiler_params=pltpu.CompilerParams(vmem_limit_bytes=HOLD_VMEM),
        cost_estimate=pl.CostEstimate(
            flops=6 * rows * width * hidden_width,
            bytes_accessed=2 * rest * hidden_width,
            transcendentals=0,
        ),
        name="experts",
    )(
        *blocks,
        in_vmem(gate_held),
        in_vmem(up_held),
        in_vmem(down_held),
        in_hbm(down_part),
        extra,
        extra,
    )


def both_terms(value):
    return value + pltpu.roll(value, LANES // 2, 1)


def add_kernel(parts, extra, kept_ref, came_ref, *outs):
    width = kept_ref.shape[1] - extra
    rows = kept_ref.shape[0] // parts
    for i in range(parts):
        mine = slice(i * rows, (i + 1) * rows)
        total = kept_ref[mine, :width].astype(jnp.float32) + came_ref[mine, :width].astype(
            jnp.float32
        )
        outs[i][:, :width] = total.astype(jnp.bfloat16)
        for at in range(width, width + extra, LANES):
            there = slice(at, at + LANES)
            total = both_terms(
                kept_ref[mine, there].astype(jnp.float32)
                + came_ref[mine, there].astype(jnp.float32)
            )
            high = total.astype(jnp.bfloat16).astype(jnp.float32)
            lane = lax.broadcasted_iota(jnp.int32, total.shape, 1)
            outs[i][:, there] = jnp.where(lane < LANES // 2, high, total - high).astype(
                jnp.bfloat16
            )


def add_parts(kept, came, parts, extra):
    rows, width = kept.shape
    out = jax.ShapeDtypeStruct((rows // parts, width), jnp.bfloat16)
    return pl.pallas_call(
        functools.partial(add_kernel, parts, extra),
        out_shape=(out,) * parts,
        compiler_params=pltpu.CompilerParams(vmem_limit_bytes=VMEM),
        cost_estimate=pl.CostEstimate(
            flops=rows * width, bytes_accessed=6 * rows * width, transcendentals=0
        ),
        name="add_slices",
    )(kept, came)


def mix_kernel(folds, weights_ref, *refs):
    out_ref, shared_out = refs[-2:]
    at = 0
    for c in range(len(refs) // EXPERTS):
        group = refs[c * EXPERTS : (c + 1) * EXPERTS]
        width = group[0].shape[1] - (folds * LANES if c == 0 else 0)
        total = weights_ref[:, 0:1] * group[0][:, :width].astype(jnp.float32)
        for k in range(1, EXPERTS):
            total = total + weights_ref[:, k : k + 1] * group[k][:, :width].astype(jnp.float32)
        out_ref[:, at : at + width] = total.astype(jnp.bfloat16)
        at += width
        if c == 0:
            rows = shared_out.shape[0] // folds
            for fold in range(folds):
                there = slice(width + fold * LANES, width + (fold + 1) * LANES)
                total = group[0][:, there].astype(jnp.float32)
                for k in range(1, EXPERTS):
                    total = total + group[k][:, there].astype(jnp.float32)
                shared_out[fold * rows : (fold + 1) * rows, :] = both_terms(total)[:rows, :ROPE]


def mix(weights, blocks, folds, shared_rows):
    rows = weights.shape[0]
    width = sum(b[0].shape[1] for b in blocks) - folds * LANES
    flat = [b for group in blocks for b in group]
    return pl.pallas_call(
        functools.partial(mix_kernel, folds),
        out_shape=(
            jax.ShapeDtypeStruct((rows, width), jnp.bfloat16),
            jax.ShapeDtypeStruct((shared_rows, ROPE), jnp.float32),
        ),
        compiler_params=pltpu.CompilerParams(vmem_limit_bytes=VMEM),
        cost_estimate=pl.CostEstimate(
            flops=8 * rows * width, bytes_accessed=10 * rows * width, transcendentals=0
        ),
        name="mix",
    )(weights, *flat)


def pass_kernel(*refs):
    del refs


def once(arrays, after):
    anywhere = pl.BlockSpec(memory_space=pl.ANY)
    count = len(arrays)
    return pl.pallas_call(
        pass_kernel,
        in_specs=[anywhere] * (count + 1),
        out_specs=(anywhere,) * count,
        out_shape=tuple(jax.ShapeDtypeStruct(a.shape, a.dtype) for a in arrays),
        input_output_aliases={i: i for i in range(count)},
        compiler_params=pltpu.CompilerParams(vmem_limit_bytes=1024 * 1024),
        cost_estimate=pl.CostEstimate(flops=0, bytes_accessed=0, transcendentals=0),
        name="once",
    )(*arrays, after)


def gathered(rows, group, after):
    came = once([swap_xor(rows, k * group) for k in range(1, EXPERTS)], after)
    blocks = {0: rows, **{k * group: came[k - 1] for k in range(1, EXPERTS)}}
    bit = 1
    while bit < group:
        for j in sorted(blocks):
            blocks[j + bit] = swap_xor(blocks[j], bit)
        bit *= 2
    return blocks


def order_of(group):
    order = [k * group for k in range(EXPERTS)]
    bit = 1
    while bit < group:
        order = order + [j + bit for j in order]
        bit *= 2
    return order


def returned(kept, sent, group, extra=0):
    bit = group // 2
    while bit > 1:
        (kept,) = add_parts(kept, swap_xor(sent, bit), 1, extra)
        kept, sent = jnp.split(kept, 2)
        bit //= 2
    parts = add_parts(kept, swap_xor(sent, 1), EXPERTS, extra)
    return [parts[0]] + [swap_xor(parts[k], k * group) for k in range(1, EXPERTS)]


def per_device(
    tokens,
    route_experts,
    route_slots,
    route_weights,
    gate_weight,
    up_weight,
    down_weight,
    query_nope,
    query_rope,
    key_nope,
    key_rope,
    value_heads,
    upstream,
):
    tokens, route_experts, route_weights = tokens[0], route_experts[0], route_weights[0]
    gate_part, up_part, down_part = gate_weight[0], up_weight[0], down_weight[0]
    model_width = tokens.shape[1]
    group = lax.axis_size("expert") // EXPERTS
    order = order_of(group)

    me = lax.axis_index("expert").astype(jnp.int32)
    width = model_width * OUT_SPLIT[0] // OUT_SPLIT[1]
    moving, extra, down_held = attention_grads(
        query_nope[0],
        query_rope[0],
        key_nope[0],
        key_rope[0],
        value_heads[0],
        upstream[0],
        me.reshape(1),
        order,
        tokens.shape[0],
        down_part,
        width,
    )
    moved = from_behind(moving, "section", -1)
    extra_moved = from_behind(extra, "section", -1)
    gate_held, up_held, hold_token = hold(gate_part, up_part, extra)
    blocks = gathered(tokens, group, hold_token)
    folds = extra.shape[1] // LANES
    kept, kept_rest, sent, sent_rest = experts(
        [blocks[j] for j in order], gate_held, up_held, down_held, down_part, extra_moved, moved
    )
    mixed = [
        returned(kept, sent, group, folds * LANES),
        returned(kept_rest, sent_rest, group),
    ]
    query_grad, key_grad, value_grad, rotary_grad = settle(
        moved, query_nope.shape[2], value_heads.shape[2], query_rope.shape[2], mixed[-1][0]
    )
    mine = me // group
    chosen = jnp.bitwise_xor(mine, jnp.arange(EXPERTS, dtype=jnp.int32))
    weights = jnp.sum(
        jnp.where(route_experts[:, :, None] == chosen, route_weights[:, :, None], 0.0), axis=1
    )
    expert_mix, shared_grad = mix(
        weights, mixed, folds, key_rope.shape[1] // lax.axis_size("expert")
    )
    return (
        expert_mix[None],
        query_grad[None],
        rotary_grad[None],
        key_grad[None],
        value_grad[None],
        shared_grad[None],
    )


def solution(mesh):
    return jax.shard_map(
        per_device,
        mesh=mesh,
        in_specs=(
            P("section", "expert", None),
            P("section", "expert", None),
            P("section", "expert", None),
            P("section", "expert", None),
            P("section", None, "expert"),
            P("section", None, "expert"),
            P("section", "expert", None),
            P("section", None, "expert"),
            P("section", None, "expert"),
            P("section", None, "expert"),
            P("section", None, None),
            P("section", None, "expert"),
            P("section", None, "expert"),
        ),
        out_specs=(
            P("section", "expert", None),
            P("section", None, "expert"),
            P("section", None, "expert"),
            P("section", None, "expert"),
            P("section", None, "expert"),
            P("section", "expert", None),
        ),
        check_vma=False,
    )
```

```python
import functools
import math

import jax
import jax.numpy as jnp
import numpy as np
from jax import lax
from jax.experimental import pallas as pl
from jax.experimental.pallas import tpu as pltpu
from jax.sharding import PartitionSpec as P

EXPERTS = 4
TOP = 2
NOPE = 128
ROPE = 64
VDIM = 128

yarn_factor = 40.0
yarn_base = 10000.0
yarn_initial = 4096.0
yarn_fast = 32.0
yarn_slow = 1.0
mask_fill = -1e30

SPLITS = (0, 1, 2)
TILE = 1024
FETCHES = 2
DOWN_TILE = 896
AFTER = False
LANES = 128
VMEM = 8 * 1024 * 1024
HELD_VMEM = 17 * 1024 * 1024


def in_hbm(array):
    return pltpu.with_memory_space_constraint(array, pltpu.HBM)


def in_vmem(array):
    return pltpu.with_memory_space_constraint(array, pltpu.VMEM)


def from_behind(array, axis, by):
    size = lax.axis_size(axis)
    pairs = [(i, i + by) for i in range(size) if 0 <= i + by < size]
    return lax.ppermute(array, axis, pairs)


def swap_xor(array, offset):
    size = lax.axis_size("expert")
    return lax.ppermute(array, "expert", [(i, i ^ offset) for i in range(size)])


def correction_point(rotations, rope_width):
    return (
        rope_width
        * math.log(yarn_initial / (rotations * 2.0 * math.pi))
        / (2.0 * math.log(yarn_base))
    )


def rotary_tables(length, rope_width):
    half_width = rope_width // 2
    lowest = max(math.floor(correction_point(yarn_fast, rope_width)), 0)
    highest = min(math.ceil(correction_point(yarn_slow, rope_width)), rope_width - 1)
    spread = np.float32(max(highest - lowest, 0.001))
    unit_index = np.arange(half_width).astype(np.float32)
    extrapolated = np.float32(1.0) / np.power(
        np.float32(yarn_base), np.float32(2.0) * unit_index / np.float32(rope_width)
    ).astype(np.float32)
    interpolated = extrapolated / np.float32(yarn_factor)
    ramp_value = np.clip((unit_index - np.float32(lowest)) / spread, 0.0, 1.0).astype(np.float32)
    frequency = interpolated * ramp_value + extrapolated * (np.float32(1.0) - ramp_value)
    angles = np.arange(length).astype(np.float32)[:, None] * frequency[None, :]
    cosine = np.cos(angles.astype(np.float64)).astype(np.float32)
    sine = np.sin(angles.astype(np.float64)).astype(np.float32)
    cosine = np.repeat(cosine, 2, axis=1)
    sine = np.repeat(sine, 2, axis=1) * np.tile(np.array([-1.0, 1.0], np.float32), half_width)
    return np.tile(cosine, (1, 2)), np.tile(sine, (1, 2))


def score_scale():
    magnitude = 0.1 * math.log(yarn_factor) + 1.0
    return (NOPE + ROPE) ** (-0.5) * magnitude * magnitude


def dot(left, right, left_dim, right_dim):
    return lax.dot_general(
        left, right, (((left_dim,), (right_dim,)), ((), ())), preferred_element_type=jnp.float32
    )


def fold_of(per_dest, block_rows):
    folds = max(per_dest // block_rows, 1)
    return folds, per_dest // folds


def extra_lanes(length, devices, folds, block_rows):
    return -(-devices * folds * block_rows // length) * LANES


def place_of(piece, length, block_rows):
    return piece * block_rows % length, piece * block_rows // length * LANES


def swap_pairs(value):
    lanes = value.shape[1]
    lane = lax.broadcasted_iota(jnp.int32, value.shape, 1)
    return jnp.where(lane % 2 == 0, pltpu.roll(value, lanes - 1, 1), pltpu.roll(value, 1, 1))


def split_moving(ref, nope, values, rope):
    widths = (nope, nope, values, rope)
    views, at = [], 0
    for width in widths:
        views.append(ref.at[:, at : at + width])
        at += width
    return views


def attention_kernel(
    query_ref,
    rope_ref,
    key_ref,
    key_rope_ref,
    value_ref,
    upstream_ref,
    cosine_ref,
    sine_ref,
    me_ref,
    moving_out,
    extra_out,
    shared_scratch,
    *,
    order,
    block_rows,
):
    length = query_ref.shape[0]
    head_count = query_ref.shape[1] // NOPE
    query_out, key_out, value_out, rotary_out = split_moving(
        moving_out, query_ref.shape[1], value_ref.shape[1], rope_ref.shape[1]
    )
    scale_value = score_scale()
    cosine = cosine_ref[...]
    sine = sine_ref[...]
    key_pair = key_rope_ref[...].astype(jnp.float32).T
    key_pair = jnp.concatenate([key_pair, key_pair], axis=1)
    key_turned = (key_pair * cosine + swap_pairs(key_pair) * sine).astype(jnp.bfloat16)
    row_pos = lax.broadcasted_iota(jnp.int32, (length, length), 0)
    col_pos = lax.broadcasted_iota(jnp.int32, (length, length), 1)
    seen = col_pos <= row_pos
    low_half = lax.broadcasted_iota(jnp.int32, (length, 2 * ROPE), 1) < ROPE
    shared = jnp.zeros((length, 2 * ROPE), jnp.float32)
    for pair in range(head_count // 2):
        both = slice(pair * 2 * ROPE, (pair + 1) * 2 * ROPE)
        rope = rope_ref[:, both].astype(jnp.float32)
        turned = rope * cosine + swap_pairs(rope) * sine
        rotary = jnp.zeros((length, 2 * ROPE), jnp.float32)
        for side in range(2):
            own = low_half if side == 0 else jnp.logical_not(low_half)
            head = slice((pair * 2 + side) * NOPE, (pair * 2 + side + 1) * NOPE)
            mine = jnp.where(own, turned, 0.0).astype(jnp.bfloat16)
            query = jnp.concatenate([query_ref[:, head], mine], axis=1)
            key = jnp.concatenate([key_ref[:, head], key_turned], axis=1)
            upstream = upstream_ref[:, head]
            scores = dot(query, key, 1, 1) * scale_value
            scores = jnp.where(seen, scores, mask_fill)
            row_top = jnp.max(scores, axis=1, keepdims=True)
            weights = jnp.exp(scores - row_top)
            softmaxed = weights / jnp.sum(weights, axis=1, keepdims=True)
            value_out[:, head] = dot(softmaxed.astype(jnp.bfloat16), upstream, 0, 0).astype(
                jnp.bfloat16
            )
            prob_grad = dot(upstream, value_ref[:, head], 1, 1)
            row_sum = jnp.sum(softmaxed * prob_grad, axis=1, keepdims=True)
            score_grad = (scale_value * softmaxed * (prob_grad - row_sum)).astype(jnp.bfloat16)
            by_query = dot(score_grad, key, 1, 0)
            by_key = dot(score_grad, query, 0, 0)
            query_out[:, head] = by_query[:, :NOPE].astype(jnp.bfloat16)
            key_out[:, head] = by_key[:, :NOPE].astype(jnp.bfloat16)
            rotary = jnp.where(own, by_query[:, NOPE:], rotary)
            shared = shared + by_key[:, NOPE:]
        rotary_out[:, both] = (rotary * cosine - swap_pairs(rotary) * sine).astype(jnp.bfloat16)
    shared = shared + pltpu.roll(shared, ROPE, 1)
    shared = shared * cosine - swap_pairs(shared) * sine
    high = shared.astype(jnp.bfloat16).astype(jnp.float32)
    shared_scratch[...] = jnp.where(low_half, high, shared - high)
    per_dest = length // len(order)
    folds, rows = fold_of(per_dest, block_rows)
    for place, index in enumerate(order):
        begin = (me_ref[0] ^ index) * per_dest
        for fold in range(folds):
            piece = shared_scratch[pl.ds(pl.multiple_of(begin + fold * rows, 8), rows), :]
            if rows < block_rows:
                piece = jnp.concatenate(
                    [piece, jnp.zeros((block_rows - rows, LANES), jnp.float32)], axis=0
                )
            row, lane = place_of(place * folds + fold, length, block_rows)
            extra_out[row : row + block_rows, lane : lane + LANES] = piece.astype(jnp.bfloat16)


def attention_grads(
    query_nope, query_rope, key_nope, key_rope, value_heads, upstream, me, order, block_rows
):
    length = query_nope.shape[0]
    cosine, sine = rotary_tables(length, ROPE)
    like = jax.ShapeDtypeStruct
    folds, _ = fold_of(length // len(order), block_rows)
    width = 2 * query_nope.shape[1] + value_heads.shape[1] + query_rope.shape[1]
    here = pl.BlockSpec(memory_space=pltpu.VMEM)
    return pl.pallas_call(
        functools.partial(attention_kernel, order=order, block_rows=block_rows),
        in_specs=[here] * 8
        + [pl.BlockSpec(memory_space=pltpu.SMEM)],
        out_specs=(here, here),
        scratch_shapes=[pltpu.VMEM((length, 2 * ROPE), jnp.float32)],
        out_shape=(
            pltpu.HBM((length, width), jnp.bfloat16),
            like(
                (length, extra_lanes(length, len(order), folds, block_rows)), jnp.bfloat16
            ),
        ),
        compiler_params=pltpu.CompilerParams(vmem_limit_bytes=HELD_VMEM),
        cost_estimate=pl.CostEstimate(
            flops=4_000_000_000, bytes_accessed=2_000_000, transcendentals=200_000
        ),
        name="attention_grads",
    )(
        in_hbm(query_nope),
        in_hbm(query_rope),
        in_hbm(key_nope),
        in_hbm(key_rope.T),
        in_hbm(value_heads),
        in_hbm(upstream),
        in_hbm(jnp.asarray(cosine)),
        in_hbm(jnp.asarray(sine)),
        me,
    )


def settle_kernel(moved_ref, after_ref, query_out, key_out, value_out, rotary_out):
    del after_ref
    views = split_moving(moved_ref, query_out.shape[1], value_out.shape[1], rotary_out.shape[1])
    for view, out in zip(views, (query_out, key_out, value_out, rotary_out)):
        out[...] = view[...]


def settle(moved, nope, values, rope, after):
    length = moved.shape[0]
    out = [jax.ShapeDtypeStruct((length, w), moved.dtype) for w in (nope, nope, values, rope)]
    return pl.pallas_call(
        settle_kernel,
        in_specs=[pl.BlockSpec(memory_space=pltpu.VMEM), pl.BlockSpec(memory_space=pl.ANY)],
        out_shape=tuple(out),
        compiler_params=pltpu.CompilerParams(vmem_limit_bytes=VMEM),
        cost_estimate=pl.CostEstimate(
            flops=0, bytes_accessed=4 * moved.size, transcendentals=0
        ),
        name="settle",
    )(in_hbm(moved), after)


def tile_of(extent, most):
    return max(t for t in range(128, most + 1, 128) if extent % t == 0)


def hold_kernel(gate_ref, up_ref, after_ref, gate_out, up_out, token_out, sems):
    del after_ref
    token_out[...] = jnp.zeros_like(token_out)
    copies = [
        pltpu.make_async_copy(gate_ref, gate_out, sems.at[0]),
        pltpu.make_async_copy(up_ref, up_out, sems.at[1]),
    ]
    for copy in copies:
        copy.start()
    for copy in copies:
        copy.wait()


def hold(gate_part, up_part, after):
    here = pl.BlockSpec(memory_space=pltpu.VMEM)
    return pl.pallas_call(
        hold_kernel,
        in_specs=[pl.BlockSpec(memory_space=pl.ANY)] * 3,
        out_specs=(here, here, here),
        out_shape=(
            pltpu.VMEM(gate_part.shape, gate_part.dtype),
            pltpu.VMEM(up_part.shape, up_part.dtype),
            jax.ShapeDtypeStruct((8, LANES), jnp.float32),
        ),
        scratch_shapes=[pltpu.SemaphoreType.DMA((2,))],
        compiler_params=pltpu.CompilerParams(vmem_limit_bytes=HELD_VMEM),
        cost_estimate=pl.CostEstimate(
            flops=0, bytes_accessed=4 * gate_part.size, transcendentals=0
        ),
        name="hold",
    )(in_hbm(gate_part), in_hbm(up_part), after)


def experts_kernel(count, folds, splits, *refs):
    blocks = refs[:count]
    gate_ref, up_ref, down_ref, extra_ref, _ = refs[count : count + 5]
    rest = refs[count + 5 :]
    parts = len(splits) - 1
    kept_refs, sent_refs, rest = rest[:parts], rest[parts : 2 * parts], rest[2 * parts :]
    gate_sum, up_sum, hidden_ref, held_ref, down_sems = rest
    width = blocks[0].shape[1]
    tile = tile_of(width, TILE)
    share = width // FETCHES
    fetches = []
    for i in range(FETCHES):
        there = slice(i * share, (i + 1) * share)
        fetches.append(
            pltpu.make_async_copy(down_ref.at[:, there], held_ref.at[:, there], down_sems.at[i])
        )
    for fetch in fetches:
        fetch.start()
    for i in range(width // tile):
        there = slice(i * tile, (i + 1) * tile)
        rows = jnp.concatenate([b[:, there] for b in blocks], axis=0)
        gate = jnp.dot(rows, gate_ref[there], preferred_element_type=jnp.float32)
        up = jnp.dot(rows, up_ref[there], preferred_element_type=jnp.float32)
        if i > 0:
            gate, up = gate_sum[...] + gate, up_sum[...] + up
        gate_sum[...] = gate
        up_sum[...] = up
    gate = gate_sum[...]
    hidden_ref[...] = (gate / (1.0 + jnp.exp(-gate)) * up_sum[...]).astype(jnp.bfloat16)
    half = hidden_ref.shape[0] // 2
    block_rows = blocks[0].shape[0]
    for piece in range(count * folds):
        row, lane = place_of(piece, extra_ref.shape[0], block_rows)
        at = piece // folds * block_rows
        out = (kept_refs if at < half else sent_refs)[0]
        begin = splits[1] + piece % folds * LANES
        out[at % half : at % half + block_rows, begin : begin + LANES] = extra_ref[
            row : row + block_rows, lane : lane + LANES
        ]
    part = 0
    tile = tile_of(share, DOWN_TILE)
    for i in range(width // tile):
        if i * tile % share == 0:
            fetches[i * tile // share].wait()
        there = slice(i * tile, (i + 1) * tile)
        out = jnp.dot(hidden_ref[...], held_ref[:, there], preferred_element_type=jnp.float32)
        while splits[part + 1] <= i * tile:
            part += 1
        mine = slice(i * tile - splits[part], (i + 1) * tile - splits[part])
        kept_refs[part][:, mine] = out[:half].astype(jnp.bfloat16)
        sent_refs[part][:, mine] = out[half:].astype(jnp.bfloat16)


def experts(blocks, gate_held, up_held, down_part, extra, folds, splits, after):
    count = len(blocks)
    block_rows, width = blocks[0].shape
    rows, hidden_width = count * block_rows, gate_held.shape[1]
    here = pl.BlockSpec(memory_space=pltpu.VMEM)
    anywhere = pl.BlockSpec(memory_space=pl.ANY)
    widths = [end - begin for begin, end in zip(splits, splits[1:])]
    widths[0] += folds * LANES
    out = [jax.ShapeDtypeStruct((rows // 2, w), jnp.bfloat16) for w in widths]
    return pl.pallas_call(
        functools.partial(experts_kernel, count, folds, splits),
        in_specs=[here] * (count + 2) + [anywhere, here, anywhere],
        out_shape=(*out, *out),
        scratch_shapes=[
            pltpu.VMEM((rows, hidden_width), jnp.float32),
            pltpu.VMEM((rows, hidden_width), jnp.float32),
            pltpu.VMEM((rows, hidden_width), jnp.bfloat16),
            pltpu.VMEM((hidden_width, width), jnp.bfloat16),
            pltpu.SemaphoreType.DMA((FETCHES,)),
        ],
        compiler_params=pltpu.CompilerParams(vmem_limit_bytes=HELD_VMEM),
        cost_estimate=pl.CostEstimate(
            flops=6 * rows * width * hidden_width,
            bytes_accessed=2 * width * hidden_width,
            transcendentals=0,
        ),
        name="experts",
    )(*blocks, in_vmem(gate_held), in_vmem(up_held), in_hbm(down_part), extra, after)


def both_terms(value):
    return value + pltpu.roll(value, LANES // 2, 1)


def add_kernel(parts, extra, kept_ref, came_ref, *outs):
    outs = outs[-parts:]
    width = kept_ref.shape[1] - extra
    rows = kept_ref.shape[0] // parts
    for i in range(parts):
        mine = slice(i * rows, (i + 1) * rows)
        total = kept_ref[mine, :width].astype(jnp.float32) + came_ref[mine, :width].astype(
            jnp.float32
        )
        outs[i][:, :width] = total.astype(jnp.bfloat16)
        for at in range(width, width + extra, LANES):
            there = slice(at, at + LANES)
            total = both_terms(
                kept_ref[mine, there].astype(jnp.float32)
                + came_ref[mine, there].astype(jnp.float32)
            )
            high = total.astype(jnp.bfloat16).astype(jnp.float32)
            lane = lax.broadcasted_iota(jnp.int32, total.shape, 1)
            outs[i][:, there] = jnp.where(lane < LANES // 2, high, total - high).astype(
                jnp.bfloat16
            )


def add_parts(kept, came, parts, extra, after=()):
    rows, width = kept.shape
    out = jax.ShapeDtypeStruct((rows // parts, width), jnp.bfloat16)
    return pl.pallas_call(
        functools.partial(add_kernel, parts, extra),
        in_specs=[pl.BlockSpec(memory_space=pltpu.VMEM)] * 2
        + [pl.BlockSpec(memory_space=pl.ANY)] * len(after),
        out_shape=(out,) * parts,
        compiler_params=pltpu.CompilerParams(vmem_limit_bytes=VMEM),
        cost_estimate=pl.CostEstimate(
            flops=rows * width, bytes_accessed=6 * rows * width, transcendentals=0
        ),
        name="add_slices",
    )(kept, came, *after)


def mix_kernel(folds, weights_ref, *refs):
    out_ref, shared_out = refs[-2:]
    at = 0
    for c in range(len(refs) // EXPERTS):
        group = refs[c * EXPERTS : (c + 1) * EXPERTS]
        width = group[0].shape[1] - (folds * LANES if c == 0 else 0)
        total = weights_ref[:, 0:1] * group[0][:, :width].astype(jnp.float32)
        for k in range(1, EXPERTS):
            total = total + weights_ref[:, k : k + 1] * group[k][:, :width].astype(jnp.float32)
        out_ref[:, at : at + width] = total.astype(jnp.bfloat16)
        at += width
        if c == 0:
            rows = shared_out.shape[0] // folds
            for fold in range(folds):
                there = slice(width + fold * LANES, width + (fold + 1) * LANES)
                total = group[0][:, there].astype(jnp.float32)
                for k in range(1, EXPERTS):
                    total = total + group[k][:, there].astype(jnp.float32)
                shared_out[fold * rows : (fold + 1) * rows, :] = both_terms(total)[:rows, :ROPE]


def mix(weights, blocks, folds, shared_rows):
    rows = weights.shape[0]
    width = sum(b[0].shape[1] for b in blocks) - folds * LANES
    flat = [b for group in blocks for b in group]
    return pl.pallas_call(
        functools.partial(mix_kernel, folds),
        out_shape=(
            jax.ShapeDtypeStruct((rows, width), jnp.bfloat16),
            jax.ShapeDtypeStruct((shared_rows, ROPE), jnp.float32),
        ),
        compiler_params=pltpu.CompilerParams(vmem_limit_bytes=VMEM),
        cost_estimate=pl.CostEstimate(
            flops=8 * rows * width, bytes_accessed=10 * rows * width, transcendentals=0
        ),
        name="mix",
    )(weights, *flat)


def pass_kernel(*refs):
    del refs


def once(arrays, after):
    anywhere = pl.BlockSpec(memory_space=pl.ANY)
    count = len(arrays)
    return pl.pallas_call(
        pass_kernel,
        in_specs=[anywhere] * (count + 1),
        out_specs=(anywhere,) * count,
        out_shape=tuple(jax.ShapeDtypeStruct(a.shape, a.dtype) for a in arrays),
        input_output_aliases={i: i for i in range(count)},
        compiler_params=pltpu.CompilerParams(vmem_limit_bytes=1024 * 1024),
        cost_estimate=pl.CostEstimate(flops=0, bytes_accessed=0, transcendentals=0),
        name="once",
    )(*arrays, after)


def gathered(rows, group, after):
    came = once([swap_xor(rows, k * group) for k in range(1, EXPERTS)], after)
    blocks = {0: rows, **{k * group: came[k - 1] for k in range(1, EXPERTS)}}
    bit = 1
    while bit < group:
        for j in sorted(blocks):
            blocks[j + bit] = swap_xor(blocks[j], bit)
        bit *= 2
    return blocks


def order_of(group):
    order = [k * group for k in range(EXPERTS)]
    bit = 1
    while bit < group:
        order = order + [j + bit for j in order]
        bit *= 2
    return order


def returned(kept, sent, group, extra=0, after=()):
    bit = group // 2
    while bit > 1:
        (kept,) = add_parts(kept, swap_xor(sent, bit), 1, extra)
        kept, sent = jnp.split(kept, 2)
        bit //= 2
    parts = add_parts(kept, swap_xor(sent, 1), EXPERTS, extra, after)
    return [parts[0]] + [swap_xor(parts[k], k * group) for k in range(1, EXPERTS)]


def per_device(
    tokens,
    route_experts,
    route_slots,
    route_weights,
    gate_weight,
    up_weight,
    down_weight,
    query_nope,
    query_rope,
    key_nope,
    key_rope,
    value_heads,
    upstream,
):
    tokens, route_experts, route_weights = tokens[0], route_experts[0], route_weights[0]
    gate_part, up_part, down_part = gate_weight[0], up_weight[0], down_weight[0]
    model_width = tokens.shape[1]
    group = lax.axis_size("expert") // EXPERTS
    order = order_of(group)

    me = lax.axis_index("expert").astype(jnp.int32)
    moving, extra = attention_grads(
        query_nope[0],
        query_rope[0],
        key_nope[0],
        key_rope[0],
        value_heads[0],
        upstream[0],
        me.reshape(1),
        order,
        tokens.shape[0],
    )
    extra_moved = from_behind(extra, "section", -1)
    moved = from_behind(moving, "section", -1)
    gate_held, up_held, token = hold(gate_part, up_part, extra)
    blocks = gathered(tokens, group, token)
    shared_rows = key_rope.shape[1] // lax.axis_size("expert")
    folds, _ = fold_of(shared_rows, tokens.shape[0])
    splits = tuple(model_width * part // SPLITS[-1] for part in SPLITS)
    outs = experts(
        [blocks[j] for j in order], gate_held, up_held, down_part, extra_moved, folds, splits, in_hbm(moved)
    )
    parts = len(splits) - 1
    mixed = [
        returned(
            outs[c],
            outs[parts + c],
            group,
            folds * LANES if c == 0 else 0,
            (in_hbm(moved),) if c == parts - 1 and AFTER else (),
        )
        for c in range(parts)
    ]
    query_grad, key_grad, value_grad, rotary_grad = settle(
        moved, query_nope.shape[2], value_heads.shape[2], query_rope.shape[2], mixed[-1][0]
    )
    mine = me // group
    chosen = jnp.bitwise_xor(mine, jnp.arange(EXPERTS, dtype=jnp.int32))
    weights = jnp.sum(
        jnp.where(route_experts[:, :, None] == chosen, route_weights[:, :, None], 0.0), axis=1
    )
    expert_mix, shared_grad = mix(weights, mixed, folds, shared_rows)
    return (
        expert_mix[None],
        query_grad[None],
        rotary_grad[None],
        key_grad[None],
        value_grad[None],
        shared_grad[None],
    )


def solution(mesh):
    return jax.shard_map(
        per_device,
        mesh=mesh,
        in_specs=(
            P("section", "expert", None),
            P("section", "expert", None),
            P("section", "expert", None),
            P("section", "expert", None),
            P("section", None, "expert"),
            P("section", None, "expert"),
            P("section", "expert", None),
            P("section", None, "expert"),
            P("section", None, "expert"),
            P("section", None, "expert"),
            P("section", None, None),
            P("section", None, "expert"),
            P("section", None, "expert"),
        ),
        out_specs=(
            P("section", "expert", None),
            P("section", None, "expert"),
            P("section", None, "expert"),
            P("section", None, "expert"),
            P("section", None, "expert"),
            P("section", "expert", None),
        ),
        check_vma=False,
    )
```

```python
import functools
import math

import jax
import jax.numpy as jnp
import numpy as np
from jax import lax
from jax.experimental import pallas as pl
from jax.experimental.pallas import tpu as pltpu
from jax.sharding import PartitionSpec as P

EXPERTS = 4
TOP = 2
NOPE = 128
ROPE = 64
VDIM = 128

yarn_factor = 40.0
yarn_base = 10000.0
yarn_initial = 4096.0
yarn_fast = 32.0
yarn_slow = 1.0
mask_fill = -1e30

SPLITS = (0, 1, 2)
TILE = 1024
FETCHES = 2
DOWN_TILE = 896
AFTER = False
LANES = 128
VMEM = 8 * 1024 * 1024
HELD_VMEM = 16 * 1024 * 1024


def in_hbm(array):
    return pltpu.with_memory_space_constraint(array, pltpu.HBM)


def in_vmem(array):
    return pltpu.with_memory_space_constraint(array, pltpu.VMEM)


def from_behind(array, axis, by):
    size = lax.axis_size(axis)
    pairs = [(i, i + by) for i in range(size) if 0 <= i + by < size]
    return lax.ppermute(array, axis, pairs)


def swap_xor(array, offset):
    size = lax.axis_size("expert")
    return lax.ppermute(array, "expert", [(i, i ^ offset) for i in range(size)])


def correction_point(rotations, rope_width):
    return (
        rope_width
        * math.log(yarn_initial / (rotations * 2.0 * math.pi))
        / (2.0 * math.log(yarn_base))
    )


def rotary_tables(length, rope_width):
    half_width = rope_width // 2
    lowest = max(math.floor(correction_point(yarn_fast, rope_width)), 0)
    highest = min(math.ceil(correction_point(yarn_slow, rope_width)), rope_width - 1)
    spread = np.float32(max(highest - lowest, 0.001))
    unit_index = np.arange(half_width).astype(np.float32)
    extrapolated = np.float32(1.0) / np.power(
        np.float32(yarn_base), np.float32(2.0) * unit_index / np.float32(rope_width)
    ).astype(np.float32)
    interpolated = extrapolated / np.float32(yarn_factor)
    ramp_value = np.clip((unit_index - np.float32(lowest)) / spread, 0.0, 1.0).astype(np.float32)
    frequency = interpolated * ramp_value + extrapolated * (np.float32(1.0) - ramp_value)
    angles = np.arange(length).astype(np.float32)[:, None] * frequency[None, :]
    cosine = np.cos(angles.astype(np.float64)).astype(np.float32)
    sine = np.sin(angles.astype(np.float64)).astype(np.float32)
    cosine = np.repeat(cosine, 2, axis=1)
    sine = np.repeat(sine, 2, axis=1) * np.tile(np.array([-1.0, 1.0], np.float32), half_width)
    return np.tile(cosine, (1, 2)), np.tile(sine, (1, 2))


def score_scale():
    magnitude = 0.1 * math.log(yarn_factor) + 1.0
    return (NOPE + ROPE) ** (-0.5) * magnitude * magnitude


def dot(left, right, left_dim, right_dim):
    return lax.dot_general(
        left, right, (((left_dim,), (right_dim,)), ((), ())), preferred_element_type=jnp.float32
    )


def fold_of(per_dest, block_rows):
    folds = max(per_dest // block_rows, 1)
    return folds, per_dest // folds


def extra_lanes(length, devices, folds, block_rows):
    return -(-devices * folds * block_rows // length) * LANES


def place_of(piece, length, block_rows):
    return piece * block_rows % length, piece * block_rows // length * LANES


def swap_pairs(value):
    lanes = value.shape[1]
    lane = lax.broadcasted_iota(jnp.int32, value.shape, 1)
    return jnp.where(lane % 2 == 0, pltpu.roll(value, lanes - 1, 1), pltpu.roll(value, 1, 1))


def split_moving(ref, nope, values, rope):
    widths = (nope, nope, values, rope)
    views, at = [], 0
    for width in widths:
        views.append(ref.at[:, at : at + width])
        at += width
    return views


def attention_kernel(
    query_ref,
    rope_ref,
    key_ref,
    key_rope_ref,
    value_ref,
    upstream_ref,
    cosine_ref,
    sine_ref,
    me_ref,
    moving_out,
    extra_out,
    shared_scratch,
    *,
    order,
    block_rows,
):
    length = query_ref.shape[0]
    head_count = query_ref.shape[1] // NOPE
    query_out, key_out, value_out, rotary_out = split_moving(
        moving_out, query_ref.shape[1], value_ref.shape[1], rope_ref.shape[1]
    )
    scale_value = score_scale()
    cosine = cosine_ref[...]
    sine = sine_ref[...]
    key_pair = key_rope_ref[...].astype(jnp.float32).T
    key_pair = jnp.concatenate([key_pair, key_pair], axis=1)
    key_turned = (key_pair * cosine + swap_pairs(key_pair) * sine).astype(jnp.bfloat16)
    row_pos = lax.broadcasted_iota(jnp.int32, (length, length), 0)
    col_pos = lax.broadcasted_iota(jnp.int32, (length, length), 1)
    seen = col_pos <= row_pos
    low_half = lax.broadcasted_iota(jnp.int32, (length, 2 * ROPE), 1) < ROPE
    shared = jnp.zeros((length, 2 * ROPE), jnp.float32)
    for pair in range(head_count // 2):
        both = slice(pair * 2 * ROPE, (pair + 1) * 2 * ROPE)
        rope = rope_ref[:, both].astype(jnp.float32)
        turned = rope * cosine + swap_pairs(rope) * sine
        rotary = jnp.zeros((length, 2 * ROPE), jnp.float32)
        for side in range(2):
            own = low_half if side == 0 else jnp.logical_not(low_half)
            head = slice((pair * 2 + side) * NOPE, (pair * 2 + side + 1) * NOPE)
            mine = jnp.where(own, turned, 0.0).astype(jnp.bfloat16)
            query = jnp.concatenate([query_ref[:, head], mine], axis=1)
            key = jnp.concatenate([key_ref[:, head], key_turned], axis=1)
            upstream = upstream_ref[:, head]
            scores = dot(query, key, 1, 1) * scale_value
            scores = jnp.where(seen, scores, mask_fill)
            row_top = jnp.max(scores, axis=1, keepdims=True)
            weights = jnp.exp(scores - row_top)
            softmaxed = weights / jnp.sum(weights, axis=1, keepdims=True)
            value_out[:, head] = dot(softmaxed.astype(jnp.bfloat16), upstream, 0, 0).astype(
                jnp.bfloat16
            )
            prob_grad = dot(upstream, value_ref[:, head], 1, 1)
            row_sum = jnp.sum(softmaxed * prob_grad, axis=1, keepdims=True)
            score_grad = (scale_value * softmaxed * (prob_grad - row_sum)).astype(jnp.bfloat16)
            by_query = dot(score_grad, key, 1, 0)
            by_key = dot(score_grad, query, 0, 0)
            query_out[:, head] = by_query[:, :NOPE].astype(jnp.bfloat16)
            key_out[:, head] = by_key[:, :NOPE].astype(jnp.bfloat16)
            rotary = jnp.where(own, by_query[:, NOPE:], rotary)
            shared = shared + by_key[:, NOPE:]
        rotary_out[:, both] = (rotary * cosine - swap_pairs(rotary) * sine).astype(jnp.bfloat16)
    shared = shared + pltpu.roll(shared, ROPE, 1)
    shared = shared * cosine - swap_pairs(shared) * sine
    high = shared.astype(jnp.bfloat16).astype(jnp.float32)
    shared_scratch[...] = jnp.where(low_half, high, shared - high)
    per_dest = length // len(order)
    folds, rows = fold_of(per_dest, block_rows)
    for place, index in enumerate(order):
        begin = (me_ref[0] ^ index) * per_dest
        for fold in range(folds):
            piece = shared_scratch[pl.ds(pl.multiple_of(begin + fold * rows, 8), rows), :]
            if rows < block_rows:
                piece = jnp.concatenate(
                    [piece, jnp.zeros((block_rows - rows, LANES), jnp.float32)], axis=0
                )
            row, lane = place_of(place * folds + fold, length, block_rows)
            extra_out[row : row + block_rows, lane : lane + LANES] = piece.astype(jnp.bfloat16)


def attention_grads(
    query_nope, query_rope, key_nope, key_rope, value_heads, upstream, me, order, block_rows
):
    length = query_nope.shape[0]
    cosine, sine = rotary_tables(length, ROPE)
    like = jax.ShapeDtypeStruct
    folds, _ = fold_of(length // len(order), block_rows)
    width = 2 * query_nope.shape[1] + value_heads.shape[1] + query_rope.shape[1]
    here = pl.BlockSpec(memory_space=pltpu.VMEM)
    return pl.pallas_call(
        functools.partial(attention_kernel, order=order, block_rows=block_rows),
        in_specs=[here] * 8
        + [pl.BlockSpec(memory_space=pltpu.SMEM)],
        out_specs=(here, here),
        scratch_shapes=[pltpu.VMEM((length, 2 * ROPE), jnp.float32)],
        out_shape=(
            like((length, width), jnp.bfloat16),
            like(
                (length, extra_lanes(length, len(order), folds, block_rows)), jnp.bfloat16
            ),
        ),
        compiler_params=pltpu.CompilerParams(vmem_limit_bytes=HELD_VMEM),
        cost_estimate=pl.CostEstimate(
            flops=4_000_000_000, bytes_accessed=2_000_000, transcendentals=200_000
        ),
        name="attention_grads",
    )(
        in_hbm(query_nope),
        in_hbm(query_rope),
        in_hbm(key_nope),
        in_hbm(key_rope.T),
        in_hbm(value_heads),
        in_hbm(upstream),
        in_hbm(jnp.asarray(cosine)),
        in_hbm(jnp.asarray(sine)),
        me,
    )


def settle_kernel(moved_ref, after_ref, query_out, key_out, value_out, rotary_out):
    del after_ref
    views = split_moving(moved_ref, query_out.shape[1], value_out.shape[1], rotary_out.shape[1])
    for view, out in zip(views, (query_out, key_out, value_out, rotary_out)):
        out[...] = view[...]


def settle(moved, nope, values, rope, after):
    length = moved.shape[0]
    out = [jax.ShapeDtypeStruct((length, w), moved.dtype) for w in (nope, nope, values, rope)]
    return pl.pallas_call(
        settle_kernel,
        in_specs=[pl.BlockSpec(memory_space=pltpu.VMEM), pl.BlockSpec(memory_space=pl.ANY)],
        out_shape=tuple(out),
        compiler_params=pltpu.CompilerParams(vmem_limit_bytes=VMEM),
        cost_estimate=pl.CostEstimate(
            flops=0, bytes_accessed=4 * moved.size, transcendentals=0
        ),
        name="settle",
    )(moved, after)


def tile_of(extent, most):
    return max(t for t in range(128, most + 1, 128) if extent % t == 0)


def hold_kernel(gate_ref, up_ref, after_ref, gate_out, up_out, token_out, sems):
    del after_ref
    token_out[...] = jnp.zeros_like(token_out)
    copies = [
        pltpu.make_async_copy(gate_ref, gate_out, sems.at[0]),
        pltpu.make_async_copy(up_ref, up_out, sems.at[1]),
    ]
    for copy in copies:
        copy.start()
    for copy in copies:
        copy.wait()


def hold(gate_part, up_part, after):
    here = pl.BlockSpec(memory_space=pltpu.VMEM)
    return pl.pallas_call(
        hold_kernel,
        in_specs=[pl.BlockSpec(memory_space=pl.ANY)] * 3,
        out_specs=(here, here, here),
        out_shape=(
            pltpu.VMEM(gate_part.shape, gate_part.dtype),
            pltpu.VMEM(up_part.shape, up_part.dtype),
            jax.ShapeDtypeStruct((8, LANES), jnp.float32),
        ),
        scratch_shapes=[pltpu.SemaphoreType.DMA((2,))],
        compiler_params=pltpu.CompilerParams(vmem_limit_bytes=HELD_VMEM),
        cost_estimate=pl.CostEstimate(
            flops=0, bytes_accessed=4 * gate_part.size, transcendentals=0
        ),
        name="hold",
    )(in_hbm(gate_part), in_hbm(up_part), after)


def experts_kernel(count, folds, splits, *refs):
    blocks = refs[:count]
    gate_ref, up_ref, down_ref, extra_ref, _ = refs[count : count + 5]
    rest = refs[count + 5 :]
    parts = len(splits) - 1
    kept_refs, sent_refs, rest = rest[:parts], rest[parts : 2 * parts], rest[2 * parts :]
    gate_sum, up_sum, hidden_ref, held_ref, down_sems = rest
    width = blocks[0].shape[1]
    tile = tile_of(width, TILE)
    share = width // FETCHES
    fetches = []
    for i in range(FETCHES):
        there = slice(i * share, (i + 1) * share)
        fetches.append(
            pltpu.make_async_copy(down_ref.at[:, there], held_ref.at[:, there], down_sems.at[i])
        )
    for fetch in fetches:
        fetch.start()
    for i in range(width // tile):
        there = slice(i * tile, (i + 1) * tile)
        rows = jnp.concatenate([b[:, there] for b in blocks], axis=0)
        gate = jnp.dot(rows, gate_ref[there], preferred_element_type=jnp.float32)
        up = jnp.dot(rows, up_ref[there], preferred_element_type=jnp.float32)
        if i > 0:
            gate, up = gate_sum[...] + gate, up_sum[...] + up
        gate_sum[...] = gate
        up_sum[...] = up
    gate = gate_sum[...]
    hidden_ref[...] = (gate / (1.0 + jnp.exp(-gate)) * up_sum[...]).astype(jnp.bfloat16)
    half = hidden_ref.shape[0] // 2
    block_rows = blocks[0].shape[0]
    for piece in range(count * folds):
        row, lane = place_of(piece, extra_ref.shape[0], block_rows)
        at = piece // folds * block_rows
        out = (kept_refs if at < half else sent_refs)[0]
        begin = splits[1] + piece % folds * LANES
        out[at % half : at % half + block_rows, begin : begin + LANES] = extra_ref[
            row : row + block_rows, lane : lane + LANES
        ]
    part = 0
    tile = tile_of(share, DOWN_TILE)
    for i in range(width // tile):
        if i * tile % share == 0:
            fetches[i * tile // share].wait()
        there = slice(i * tile, (i + 1) * tile)
        out = jnp.dot(hidden_ref[...], held_ref[:, there], preferred_element_type=jnp.float32)
        while splits[part + 1] <= i * tile:
            part += 1
        mine = slice(i * tile - splits[part], (i + 1) * tile - splits[part])
        kept_refs[part][:, mine] = out[:half].astype(jnp.bfloat16)
        sent_refs[part][:, mine] = out[half:].astype(jnp.bfloat16)


def experts(blocks, gate_held, up_held, down_part, extra, folds, splits, after):
    count = len(blocks)
    block_rows, width = blocks[0].shape
    rows, hidden_width = count * block_rows, gate_held.shape[1]
    here = pl.BlockSpec(memory_space=pltpu.VMEM)
    anywhere = pl.BlockSpec(memory_space=pl.ANY)
    widths = [end - begin for begin, end in zip(splits, splits[1:])]
    widths[0] += folds * LANES
    out = [jax.ShapeDtypeStruct((rows // 2, w), jnp.bfloat16) for w in widths]
    return pl.pallas_call(
        functools.partial(experts_kernel, count, folds, splits),
        in_specs=[here] * (count + 2) + [anywhere, here, anywhere],
        out_shape=(*out, *out),
        scratch_shapes=[
            pltpu.VMEM((rows, hidden_width), jnp.float32),
            pltpu.VMEM((rows, hidden_width), jnp.float32),
            pltpu.VMEM((rows, hidden_width), jnp.bfloat16),
            pltpu.VMEM((hidden_width, width), jnp.bfloat16),
            pltpu.SemaphoreType.DMA((FETCHES,)),
        ],
        compiler_params=pltpu.CompilerParams(vmem_limit_bytes=HELD_VMEM),
        cost_estimate=pl.CostEstimate(
            flops=6 * rows * width * hidden_width,
            bytes_accessed=2 * width * hidden_width,
            transcendentals=0,
        ),
        name="experts",
    )(*blocks, in_vmem(gate_held), in_vmem(up_held), in_hbm(down_part), extra, after)


def both_terms(value):
    return value + pltpu.roll(value, LANES // 2, 1)


def add_kernel(parts, extra, kept_ref, came_ref, *outs):
    outs = outs[-parts:]
    width = kept_ref.shape[1] - extra
    rows = kept_ref.shape[0] // parts
    for i in range(parts):
        mine = slice(i * rows, (i + 1) * rows)
        total = kept_ref[mine, :width].astype(jnp.float32) + came_ref[mine, :width].astype(
            jnp.float32
        )
        outs[i][:, :width] = total.astype(jnp.bfloat16)
        for at in range(width, width + extra, LANES):
            there = slice(at, at + LANES)
            total = both_terms(
                kept_ref[mine, there].astype(jnp.float32)
                + came_ref[mine, there].astype(jnp.float32)
            )
            high = total.astype(jnp.bfloat16).astype(jnp.float32)
            lane = lax.broadcasted_iota(jnp.int32, total.shape, 1)
            outs[i][:, there] = jnp.where(lane < LANES // 2, high, total - high).astype(
                jnp.bfloat16
            )


def add_parts(kept, came, parts, extra, after=()):
    rows, width = kept.shape
    out = jax.ShapeDtypeStruct((rows // parts, width), jnp.bfloat16)
    return pl.pallas_call(
        functools.partial(add_kernel, parts, extra),
        in_specs=[pl.BlockSpec(memory_space=pltpu.VMEM)] * 2
        + [pl.BlockSpec(memory_space=pl.ANY)] * len(after),
        out_shape=(out,) * parts,
        compiler_params=pltpu.CompilerParams(vmem_limit_bytes=VMEM),
        cost_estimate=pl.CostEstimate(
            flops=rows * width, bytes_accessed=6 * rows * width, transcendentals=0
        ),
        name="add_slices",
    )(kept, came, *after)


def mix_kernel(folds, weights_ref, *refs):
    out_ref, shared_out = refs[-2:]
    at = 0
    for c in range(len(refs) // EXPERTS):
        group = refs[c * EXPERTS : (c + 1) * EXPERTS]
        width = group[0].shape[1] - (folds * LANES if c == 0 else 0)
        total = weights_ref[:, 0:1] * group[0][:, :width].astype(jnp.float32)
        for k in range(1, EXPERTS):
            total = total + weights_ref[:, k : k + 1] * group[k][:, :width].astype(jnp.float32)
        out_ref[:, at : at + width] = total.astype(jnp.bfloat16)
        at += width
        if c == 0:
            rows = shared_out.shape[0] // folds
            for fold in range(folds):
                there = slice(width + fold * LANES, width + (fold + 1) * LANES)
                total = group[0][:, there].astype(jnp.float32)
                for k in range(1, EXPERTS):
                    total = total + group[k][:, there].astype(jnp.float32)
                shared_out[fold * rows : (fold + 1) * rows, :] = both_terms(total)[:rows, :ROPE]


def mix(weights, blocks, folds, shared_rows):
    rows = weights.shape[0]
    width = sum(b[0].shape[1] for b in blocks) - folds * LANES
    flat = [b for group in blocks for b in group]
    return pl.pallas_call(
        functools.partial(mix_kernel, folds),
        out_shape=(
            jax.ShapeDtypeStruct((rows, width), jnp.bfloat16),
            jax.ShapeDtypeStruct((shared_rows, ROPE), jnp.float32),
        ),
        compiler_params=pltpu.CompilerParams(vmem_limit_bytes=VMEM),
        cost_estimate=pl.CostEstimate(
            flops=8 * rows * width, bytes_accessed=10 * rows * width, transcendentals=0
        ),
        name="mix",
    )(weights, *flat)


def pass_kernel(*refs):
    del refs


def once(arrays, after):
    anywhere = pl.BlockSpec(memory_space=pl.ANY)
    count = len(arrays)
    return pl.pallas_call(
        pass_kernel,
        in_specs=[anywhere] * (count + 1),
        out_specs=(anywhere,) * count,
        out_shape=tuple(jax.ShapeDtypeStruct(a.shape, a.dtype) for a in arrays),
        input_output_aliases={i: i for i in range(count)},
        compiler_params=pltpu.CompilerParams(vmem_limit_bytes=1024 * 1024),
        cost_estimate=pl.CostEstimate(flops=0, bytes_accessed=0, transcendentals=0),
        name="once",
    )(*arrays, after)


def gathered(rows, group, after):
    came = once([swap_xor(rows, k * group) for k in range(1, EXPERTS)], after)
    blocks = {0: rows, **{k * group: came[k - 1] for k in range(1, EXPERTS)}}
    bit = 1
    while bit < group:
        for j in sorted(blocks):
            blocks[j + bit] = swap_xor(blocks[j], bit)
        bit *= 2
    return blocks


def order_of(group):
    order = [k * group for k in range(EXPERTS)]
    bit = 1
    while bit < group:
        order = order + [j + bit for j in order]
        bit *= 2
    return order


def returned(kept, sent, group, extra=0, after=()):
    bit = group // 2
    while bit > 1:
        (kept,) = add_parts(kept, swap_xor(sent, bit), 1, extra)
        kept, sent = jnp.split(kept, 2)
        bit //= 2
    parts = add_parts(kept, swap_xor(sent, 1), EXPERTS, extra, after)
    return [parts[0]] + [swap_xor(parts[k], k * group) for k in range(1, EXPERTS)]


def per_device(
    tokens,
    route_experts,
    route_slots,
    route_weights,
    gate_weight,
    up_weight,
    down_weight,
    query_nope,
    query_rope,
    key_nope,
    key_rope,
    value_heads,
    upstream,
):
    tokens, route_experts, route_weights = tokens[0], route_experts[0], route_weights[0]
    gate_part, up_part, down_part = gate_weight[0], up_weight[0], down_weight[0]
    model_width = tokens.shape[1]
    group = lax.axis_size("expert") // EXPERTS
    order = order_of(group)

    me = lax.axis_index("expert").astype(jnp.int32)
    moving, extra = attention_grads(
        query_nope[0],
        query_rope[0],
        key_nope[0],
        key_rope[0],
        value_heads[0],
        upstream[0],
        me.reshape(1),
        order,
        tokens.shape[0],
    )
    extra_moved = from_behind(extra, "section", -1)
    moved = from_behind(moving, "section", -1)
    gate_held, up_held, token = hold(gate_part, up_part, extra)
    blocks = gathered(tokens, group, token)
    shared_rows = key_rope.shape[1] // lax.axis_size("expert")
    folds, _ = fold_of(shared_rows, tokens.shape[0])
    splits = tuple(model_width * part // SPLITS[-1] for part in SPLITS)
    outs = experts(
        [blocks[j] for j in order], gate_held, up_held, down_part, extra_moved, folds, splits, moved
    )
    parts = len(splits) - 1
    mixed = [
        returned(
            outs[c],
            outs[parts + c],
            group,
            folds * LANES if c == 0 else 0,
            (in_hbm(moved),) if c == parts - 1 and AFTER else (),
        )
        for c in range(parts)
    ]
    query_grad, key_grad, value_grad, rotary_grad = settle(
        moved, query_nope.shape[2], value_heads.shape[2], query_rope.shape[2], mixed[-1][0]
    )
    mine = me // group
    chosen = jnp.bitwise_xor(mine, jnp.arange(EXPERTS, dtype=jnp.int32))
    weights = jnp.sum(
        jnp.where(route_experts[:, :, None] == chosen, route_weights[:, :, None], 0.0), axis=1
    )
    expert_mix, shared_grad = mix(weights, mixed, folds, shared_rows)
    return (
        expert_mix[None],
        query_grad[None],
        rotary_grad[None],
        key_grad[None],
        value_grad[None],
        shared_grad[None],
    )


def solution(mesh):
    return jax.shard_map(
        per_device,
        mesh=mesh,
        in_specs=(
            P("section", "expert", None),
            P("section", "expert", None),
            P("section", "expert", None),
            P("section", "expert", None),
            P("section", None, "expert"),
            P("section", None, "expert"),
            P("section", "expert", None),
            P("section", None, "expert"),
            P("section", None, "expert"),
            P("section", None, "expert"),
            P("section", None, None),
            P("section", None, "expert"),
            P("section", None, "expert"),
        ),
        out_specs=(
            P("section", "expert", None),
            P("section", None, "expert"),
            P("section", None, "expert"),
            P("section", None, "expert"),
            P("section", None, "expert"),
            P("section", "expert", None),
        ),
        check_vma=False,
    )
```

```python
import functools
import math

import jax
import jax.numpy as jnp
import numpy as np
from jax import lax
from jax.experimental import pallas as pl
from jax.experimental.pallas import tpu as pltpu
from jax.sharding import PartitionSpec as P

EXPERTS = 4
TOP = 2
NOPE = 128
ROPE = 64
VDIM = 128

yarn_factor = 40.0
yarn_base = 10000.0
yarn_initial = 4096.0
yarn_fast = 32.0
yarn_slow = 1.0
mask_fill = -1e30

SPLITS = (0, 1, 2)
TILE = 1024
DOWN_TILE = 896
AFTER = False
LANES = 128
VMEM = 8 * 1024 * 1024
HELD_VMEM = 9 * 1024 * 1024


def in_hbm(array):
    return pltpu.with_memory_space_constraint(array, pltpu.HBM)


def in_vmem(array):
    return pltpu.with_memory_space_constraint(array, pltpu.VMEM)


def from_behind(array, axis, by):
    size = lax.axis_size(axis)
    pairs = [(i, i + by) for i in range(size) if 0 <= i + by < size]
    return lax.ppermute(array, axis, pairs)


def swap_xor(array, offset):
    size = lax.axis_size("expert")
    return lax.ppermute(array, "expert", [(i, i ^ offset) for i in range(size)])


def correction_point(rotations, rope_width):
    return (
        rope_width
        * math.log(yarn_initial / (rotations * 2.0 * math.pi))
        / (2.0 * math.log(yarn_base))
    )


def rotary_tables(length, rope_width):
    half_width = rope_width // 2
    lowest = max(math.floor(correction_point(yarn_fast, rope_width)), 0)
    highest = min(math.ceil(correction_point(yarn_slow, rope_width)), rope_width - 1)
    spread = np.float32(max(highest - lowest, 0.001))
    unit_index = np.arange(half_width).astype(np.float32)
    extrapolated = np.float32(1.0) / np.power(
        np.float32(yarn_base), np.float32(2.0) * unit_index / np.float32(rope_width)
    ).astype(np.float32)
    interpolated = extrapolated / np.float32(yarn_factor)
    ramp_value = np.clip((unit_index - np.float32(lowest)) / spread, 0.0, 1.0).astype(np.float32)
    frequency = interpolated * ramp_value + extrapolated * (np.float32(1.0) - ramp_value)
    angles = np.arange(length).astype(np.float32)[:, None] * frequency[None, :]
    cosine = np.cos(angles.astype(np.float64)).astype(np.float32)
    sine = np.sin(angles.astype(np.float64)).astype(np.float32)
    cosine = np.repeat(cosine, 2, axis=1)
    sine = np.repeat(sine, 2, axis=1) * np.tile(np.array([-1.0, 1.0], np.float32), half_width)
    return np.tile(cosine, (1, 2)), np.tile(sine, (1, 2))


def score_scale():
    magnitude = 0.1 * math.log(yarn_factor) + 1.0
    return (NOPE + ROPE) ** (-0.5) * magnitude * magnitude


def dot(left, right, left_dim, right_dim):
    return lax.dot_general(
        left, right, (((left_dim,), (right_dim,)), ((), ())), preferred_element_type=jnp.float32
    )


def fold_of(per_dest, block_rows):
    folds = max(per_dest // block_rows, 1)
    return folds, per_dest // folds


def extra_lanes(length, devices, folds, block_rows):
    return -(-devices * folds * block_rows // length) * LANES


def place_of(piece, length, block_rows):
    return piece * block_rows % length, piece * block_rows // length * LANES


def swap_pairs(value):
    lanes = value.shape[1]
    lane = lax.broadcasted_iota(jnp.int32, value.shape, 1)
    return jnp.where(lane % 2 == 0, pltpu.roll(value, lanes - 1, 1), pltpu.roll(value, 1, 1))


def split_moving(ref, nope, values, rope):
    widths = (nope, nope, values, rope)
    views, at = [], 0
    for width in widths:
        views.append(ref.at[:, at : at + width])
        at += width
    return views


def attention_kernel(
    query_ref,
    rope_ref,
    key_ref,
    key_rope_ref,
    value_ref,
    upstream_ref,
    cosine_ref,
    sine_ref,
    me_ref,
    moving_out,
    extra_out,
    shared_scratch,
    *,
    order,
    block_rows,
):
    length = query_ref.shape[0]
    head_count = query_ref.shape[1] // NOPE
    query_out, key_out, value_out, rotary_out = split_moving(
        moving_out, query_ref.shape[1], value_ref.shape[1], rope_ref.shape[1]
    )
    scale_value = score_scale()
    cosine = cosine_ref[...]
    sine = sine_ref[...]
    key_pair = key_rope_ref[...].astype(jnp.float32).T
    key_pair = jnp.concatenate([key_pair, key_pair], axis=1)
    key_turned = (key_pair * cosine + swap_pairs(key_pair) * sine).astype(jnp.bfloat16)
    row_pos = lax.broadcasted_iota(jnp.int32, (length, length), 0)
    col_pos = lax.broadcasted_iota(jnp.int32, (length, length), 1)
    seen = col_pos <= row_pos
    low_half = lax.broadcasted_iota(jnp.int32, (length, 2 * ROPE), 1) < ROPE
    shared = jnp.zeros((length, 2 * ROPE), jnp.float32)
    for pair in range(head_count // 2):
        both = slice(pair * 2 * ROPE, (pair + 1) * 2 * ROPE)
        rope = rope_ref[:, both].astype(jnp.float32)
        turned = rope * cosine + swap_pairs(rope) * sine
        rotary = jnp.zeros((length, 2 * ROPE), jnp.float32)
        for side in range(2):
            own = low_half if side == 0 else jnp.logical_not(low_half)
            head = slice((pair * 2 + side) * NOPE, (pair * 2 + side + 1) * NOPE)
            mine = jnp.where(own, turned, 0.0).astype(jnp.bfloat16)
            query = jnp.concatenate([query_ref[:, head], mine], axis=1)
            key = jnp.concatenate([key_ref[:, head], key_turned], axis=1)
            upstream = upstream_ref[:, head]
            scores = dot(query, key, 1, 1) * scale_value
            scores = jnp.where(seen, scores, mask_fill)
            row_top = jnp.max(scores, axis=1, keepdims=True)
            weights = jnp.exp(scores - row_top)
            softmaxed = weights / jnp.sum(weights, axis=1, keepdims=True)
            value_out[:, head] = dot(softmaxed.astype(jnp.bfloat16), upstream, 0, 0).astype(
                jnp.bfloat16
            )
            prob_grad = dot(upstream, value_ref[:, head], 1, 1)
            row_sum = jnp.sum(softmaxed * prob_grad, axis=1, keepdims=True)
            score_grad = (scale_value * softmaxed * (prob_grad - row_sum)).astype(jnp.bfloat16)
            by_query = dot(score_grad, key, 1, 0)
            by_key = dot(score_grad, query, 0, 0)
            query_out[:, head] = by_query[:, :NOPE].astype(jnp.bfloat16)
            key_out[:, head] = by_key[:, :NOPE].astype(jnp.bfloat16)
            rotary = jnp.where(own, by_query[:, NOPE:], rotary)
            shared = shared + by_key[:, NOPE:]
        rotary_out[:, both] = (rotary * cosine - swap_pairs(rotary) * sine).astype(jnp.bfloat16)
    shared = shared + pltpu.roll(shared, ROPE, 1)
    shared = shared * cosine - swap_pairs(shared) * sine
    high = shared.astype(jnp.bfloat16).astype(jnp.float32)
    shared_scratch[...] = jnp.where(low_half, high, shared - high)
    per_dest = length // len(order)
    folds, rows = fold_of(per_dest, block_rows)
    for place, index in enumerate(order):
        begin = (me_ref[0] ^ index) * per_dest
        for fold in range(folds):
            piece = shared_scratch[pl.ds(pl.multiple_of(begin + fold * rows, 8), rows), :]
            if rows < block_rows:
                piece = jnp.concatenate(
                    [piece, jnp.zeros((block_rows - rows, LANES), jnp.float32)], axis=0
                )
            row, lane = place_of(place * folds + fold, length, block_rows)
            extra_out[row : row + block_rows, lane : lane + LANES] = piece.astype(jnp.bfloat16)


def attention_grads(
    query_nope, query_rope, key_nope, key_rope, value_heads, upstream, me, order, block_rows
):
    length = query_nope.shape[0]
    cosine, sine = rotary_tables(length, ROPE)
    like = jax.ShapeDtypeStruct
    folds, _ = fold_of(length // len(order), block_rows)
    width = 2 * query_nope.shape[1] + value_heads.shape[1] + query_rope.shape[1]
    here = pl.BlockSpec(memory_space=pltpu.VMEM)
    return pl.pallas_call(
        functools.partial(attention_kernel, order=order, block_rows=block_rows),
        in_specs=[here] * 8
        + [pl.BlockSpec(memory_space=pltpu.SMEM)],
        out_specs=(here, here),
        scratch_shapes=[pltpu.VMEM((length, 2 * ROPE), jnp.float32)],
        out_shape=(
            like((length, width), jnp.bfloat16),
            like(
                (length, extra_lanes(length, len(order), folds, block_rows)), jnp.bfloat16
            ),
        ),
        compiler_params=pltpu.CompilerParams(vmem_limit_bytes=HELD_VMEM),
        cost_estimate=pl.CostEstimate(
            flops=4_000_000_000, bytes_accessed=2_000_000, transcendentals=200_000
        ),
        name="attention_grads",
    )(
        in_hbm(query_nope),
        in_hbm(query_rope),
        in_hbm(key_nope),
        in_hbm(key_rope.T),
        in_hbm(value_heads),
        in_hbm(upstream),
        in_hbm(jnp.asarray(cosine)),
        in_hbm(jnp.asarray(sine)),
        me,
    )


def settle_kernel(moved_ref, after_ref, query_out, key_out, value_out, rotary_out):
    del after_ref
    views = split_moving(moved_ref, query_out.shape[1], value_out.shape[1], rotary_out.shape[1])
    for view, out in zip(views, (query_out, key_out, value_out, rotary_out)):
        out[...] = view[...]


def settle(moved, nope, values, rope, after):
    length = moved.shape[0]
    out = [jax.ShapeDtypeStruct((length, w), moved.dtype) for w in (nope, nope, values, rope)]
    return pl.pallas_call(
        settle_kernel,
        in_specs=[pl.BlockSpec(memory_space=pltpu.VMEM), pl.BlockSpec(memory_space=pl.ANY)],
        out_shape=tuple(out),
        compiler_params=pltpu.CompilerParams(vmem_limit_bytes=VMEM),
        cost_estimate=pl.CostEstimate(
            flops=0, bytes_accessed=4 * moved.size, transcendentals=0
        ),
        name="settle",
    )(moved, after)


def tile_of(extent, most):
    return max(t for t in range(128, most + 1, 128) if extent % t == 0)


def hold_kernel(up_ref, down_ref, after_ref, up_out, down_out, token_out, sems):
    del after_ref
    token_out[...] = jnp.zeros_like(token_out)
    copies = [
        pltpu.make_async_copy(up_ref, up_out, sems.at[0]),
        pltpu.make_async_copy(down_ref.at[:, : down_out.shape[1]], down_out, sems.at[1]),
    ]
    for copy in copies:
        copy.start()
    for copy in copies:
        copy.wait()


def hold(up_part, down_part, width, after):
    here = pl.BlockSpec(memory_space=pltpu.VMEM)
    return pl.pallas_call(
        hold_kernel,
        in_specs=[pl.BlockSpec(memory_space=pl.ANY)] * 3,
        out_specs=(here, here, here),
        out_shape=(
            pltpu.VMEM(up_part.shape, up_part.dtype),
            pltpu.VMEM((down_part.shape[0], width), down_part.dtype),
            jax.ShapeDtypeStruct((8, LANES), jnp.float32),
        ),
        scratch_shapes=[pltpu.SemaphoreType.DMA((2,))],
        compiler_params=pltpu.CompilerParams(vmem_limit_bytes=HELD_VMEM),
        cost_estimate=pl.CostEstimate(
            flops=0, bytes_accessed=2 * up_part.size, transcendentals=0
        ),
        name="hold",
    )(in_hbm(up_part), in_hbm(down_part), after)


def experts_kernel(count, folds, splits, *refs):
    blocks = refs[:count]
    gate_ref, up_ref, first_ref, down_ref, extra_ref, _ = refs[count : count + 6]
    rest = refs[count + 6 :]
    parts = len(splits) - 1
    kept_refs, sent_refs, rest = rest[:parts], rest[parts : 2 * parts], rest[2 * parts :]
    gate_sum, up_sum, hidden_ref, rest_ref, down_sem = rest
    width = blocks[0].shape[1]
    tile = tile_of(width, TILE)
    share = first_ref.shape[1]
    fetch = pltpu.make_async_copy(down_ref.at[:, share:], rest_ref, down_sem)
    fetch.start()
    for i in range(width // tile):
        there = slice(i * tile, (i + 1) * tile)
        rows = jnp.concatenate([b[:, there] for b in blocks], axis=0)
        gate = jnp.dot(rows, gate_ref[there], preferred_element_type=jnp.float32)
        up = jnp.dot(rows, up_ref[there], preferred_element_type=jnp.float32)
        if i > 0:
            gate, up = gate_sum[...] + gate, up_sum[...] + up
        gate_sum[...] = gate
        up_sum[...] = up
    gate = gate_sum[...]
    hidden_ref[...] = (gate / (1.0 + jnp.exp(-gate)) * up_sum[...]).astype(jnp.bfloat16)
    half = hidden_ref.shape[0] // 2
    block_rows = blocks[0].shape[0]
    for piece in range(count * folds):
        row, lane = place_of(piece, extra_ref.shape[0], block_rows)
        at = piece // folds * block_rows
        out = (kept_refs if at < half else sent_refs)[0]
        begin = splits[1] + piece % folds * LANES
        out[at % half : at % half + block_rows, begin : begin + LANES] = extra_ref[
            row : row + block_rows, lane : lane + LANES
        ]
    part = 0
    tile = tile_of(share, DOWN_TILE)
    for i in range(width // tile):
        if i * tile == share:
            fetch.wait()
        weights, back = (first_ref, 0) if i * tile < share else (rest_ref, share)
        out = jnp.dot(hidden_ref[...], weights[:, i * tile - back : (i + 1) * tile - back], preferred_element_type=jnp.float32)
        while splits[part + 1] <= i * tile:
            part += 1
        mine = slice(i * tile - splits[part], (i + 1) * tile - splits[part])
        kept_refs[part][:, mine] = out[:half].astype(jnp.bfloat16)
        sent_refs[part][:, mine] = out[half:].astype(jnp.bfloat16)


def experts(blocks, gate_held, up_held, down_held, down_part, extra, folds, splits, after):
    count = len(blocks)
    block_rows, width = blocks[0].shape
    rows, hidden_width = count * block_rows, gate_held.shape[1]
    here = pl.BlockSpec(memory_space=pltpu.VMEM)
    anywhere = pl.BlockSpec(memory_space=pl.ANY)
    widths = [end - begin for begin, end in zip(splits, splits[1:])]
    widths[0] += folds * LANES
    out = [jax.ShapeDtypeStruct((rows // 2, w), jnp.bfloat16) for w in widths]
    return pl.pallas_call(
        functools.partial(experts_kernel, count, folds, splits),
        in_specs=[here] * (count + 3) + [anywhere, here, anywhere],
        out_shape=(*out, *out),
        scratch_shapes=[
            pltpu.VMEM((rows, hidden_width), jnp.float32),
            pltpu.VMEM((rows, hidden_width), jnp.float32),
            pltpu.VMEM((rows, hidden_width), jnp.bfloat16),
            pltpu.VMEM((hidden_width, width - down_held.shape[1]), jnp.bfloat16),
            pltpu.SemaphoreType.DMA(()),
        ],
        compiler_params=pltpu.CompilerParams(vmem_limit_bytes=HELD_VMEM),
        cost_estimate=pl.CostEstimate(
            flops=6 * rows * width * hidden_width,
            bytes_accessed=2 * width * hidden_width,
            transcendentals=0,
        ),
        name="experts",
    )(*blocks, in_vmem(gate_held), in_vmem(up_held), in_vmem(down_held), in_hbm(down_part), extra, after)


def both_terms(value):
    return value + pltpu.roll(value, LANES // 2, 1)


def add_kernel(parts, extra, kept_ref, came_ref, *outs):
    outs = outs[-parts:]
    width = kept_ref.shape[1] - extra
    rows = kept_ref.shape[0] // parts
    for i in range(parts):
        mine = slice(i * rows, (i + 1) * rows)
        total = kept_ref[mine, :width].astype(jnp.float32) + came_ref[mine, :width].astype(
            jnp.float32
        )
        outs[i][:, :width] = total.astype(jnp.bfloat16)
        for at in range(width, width + extra, LANES):
            there = slice(at, at + LANES)
            total = both_terms(
                kept_ref[mine, there].astype(jnp.float32)
                + came_ref[mine, there].astype(jnp.float32)
            )
            high = total.astype(jnp.bfloat16).astype(jnp.float32)
            lane = lax.broadcasted_iota(jnp.int32, total.shape, 1)
            outs[i][:, there] = jnp.where(lane < LANES // 2, high, total - high).astype(
                jnp.bfloat16
            )


def add_parts(kept, came, parts, extra, after=()):
    rows, width = kept.shape
    out = jax.ShapeDtypeStruct((rows // parts, width), jnp.bfloat16)
    return pl.pallas_call(
        functools.partial(add_kernel, parts, extra),
        in_specs=[pl.BlockSpec(memory_space=pltpu.VMEM)] * 2
        + [pl.BlockSpec(memory_space=pl.ANY)] * len(after),
        out_shape=(out,) * parts,
        compiler_params=pltpu.CompilerParams(vmem_limit_bytes=VMEM),
        cost_estimate=pl.CostEstimate(
            flops=rows * width, bytes_accessed=6 * rows * width, transcendentals=0
        ),
        name="add_slices",
    )(kept, came, *after)


def mix_kernel(folds, weights_ref, *refs):
    out_ref, shared_out = refs[-2:]
    at = 0
    for c in range(len(refs) // EXPERTS):
        group = refs[c * EXPERTS : (c + 1) * EXPERTS]
        width = group[0].shape[1] - (folds * LANES if c == 0 else 0)
        total = weights_ref[:, 0:1] * group[0][:, :width].astype(jnp.float32)
        for k in range(1, EXPERTS):
            total = total + weights_ref[:, k : k + 1] * group[k][:, :width].astype(jnp.float32)
        out_ref[:, at : at + width] = total.astype(jnp.bfloat16)
        at += width
        if c == 0:
            rows = shared_out.shape[0] // folds
            for fold in range(folds):
                there = slice(width + fold * LANES, width + (fold + 1) * LANES)
                total = group[0][:, there].astype(jnp.float32)
                for k in range(1, EXPERTS):
                    total = total + group[k][:, there].astype(jnp.float32)
                shared_out[fold * rows : (fold + 1) * rows, :] = both_terms(total)[:rows, :ROPE]


def mix(weights, blocks, folds, shared_rows):
    rows = weights.shape[0]
    width = sum(b[0].shape[1] for b in blocks) - folds * LANES
    flat = [b for group in blocks for b in group]
    return pl.pallas_call(
        functools.partial(mix_kernel, folds),
        out_shape=(
            jax.ShapeDtypeStruct((rows, width), jnp.bfloat16),
            jax.ShapeDtypeStruct((shared_rows, ROPE), jnp.float32),
        ),
        compiler_params=pltpu.CompilerParams(vmem_limit_bytes=VMEM),
        cost_estimate=pl.CostEstimate(
            flops=8 * rows * width, bytes_accessed=10 * rows * width, transcendentals=0
        ),
        name="mix",
    )(weights, *flat)


def pass_kernel(*refs):
    del refs


def once(arrays, after):
    anywhere = pl.BlockSpec(memory_space=pl.ANY)
    count = len(arrays)
    return pl.pallas_call(
        pass_kernel,
        in_specs=[anywhere] * (count + 1),
        out_specs=(anywhere,) * count,
        out_shape=tuple(jax.ShapeDtypeStruct(a.shape, a.dtype) for a in arrays),
        input_output_aliases={i: i for i in range(count)},
        compiler_params=pltpu.CompilerParams(vmem_limit_bytes=1024 * 1024),
        cost_estimate=pl.CostEstimate(flops=0, bytes_accessed=0, transcendentals=0),
        name="once",
    )(*arrays, after)


def gathered(rows, group, after):
    came = once([swap_xor(rows, k * group) for k in range(1, EXPERTS)], after)
    blocks = {0: rows, **{k * group: came[k - 1] for k in range(1, EXPERTS)}}
    bit = 1
    while bit < group:
        for j in sorted(blocks):
            blocks[j + bit] = swap_xor(blocks[j], bit)
        bit *= 2
    return blocks


def order_of(group):
    order = [k * group for k in range(EXPERTS)]
    bit = 1
    while bit < group:
        order = order + [j + bit for j in order]
        bit *= 2
    return order


def returned(kept, sent, group, extra=0, after=()):
    bit = group // 2
    while bit > 1:
        (kept,) = add_parts(kept, swap_xor(sent, bit), 1, extra)
        kept, sent = jnp.split(kept, 2)
        bit //= 2
    parts = add_parts(kept, swap_xor(sent, 1), EXPERTS, extra, after)
    return [parts[0]] + [swap_xor(parts[k], k * group) for k in range(1, EXPERTS)]


def per_device(
    tokens,
    route_experts,
    route_slots,
    route_weights,
    gate_weight,
    up_weight,
    down_weight,
    query_nope,
    query_rope,
    key_nope,
    key_rope,
    value_heads,
    upstream,
):
    tokens, route_experts, route_weights = tokens[0], route_experts[0], route_weights[0]
    gate_part, up_part, down_part = gate_weight[0], up_weight[0], down_weight[0]
    model_width = tokens.shape[1]
    group = lax.axis_size("expert") // EXPERTS
    order = order_of(group)

    me = lax.axis_index("expert").astype(jnp.int32)
    moving, extra = attention_grads(
        query_nope[0],
        query_rope[0],
        key_nope[0],
        key_rope[0],
        value_heads[0],
        upstream[0],
        me.reshape(1),
        order,
        tokens.shape[0],
    )
    extra_moved = from_behind(extra, "section", -1)
    moved = from_behind(moving, "section", -1)
    up_held, down_held, token = hold(
        up_part, down_part, model_width // 2, extra
    )
    gate_held = gate_part
    blocks = gathered(tokens, group, token)
    shared_rows = key_rope.shape[1] // lax.axis_size("expert")
    folds, _ = fold_of(shared_rows, tokens.shape[0])
    splits = tuple(model_width * part // SPLITS[-1] for part in SPLITS)
    outs = experts(
        [blocks[j] for j in order], gate_held, up_held, down_held, down_part, extra_moved, folds, splits, moved
    )
    parts = len(splits) - 1
    mixed = [
        returned(
            outs[c],
            outs[parts + c],
            group,
            folds * LANES if c == 0 else 0,
            (in_hbm(moved),) if c == parts - 1 and AFTER else (),
        )
        for c in range(parts)
    ]
    query_grad, key_grad, value_grad, rotary_grad = settle(
        moved, query_nope.shape[2], value_heads.shape[2], query_rope.shape[2], mixed[-1][0]
    )
    mine = me // group
    chosen = jnp.bitwise_xor(mine, jnp.arange(EXPERTS, dtype=jnp.int32))
    weights = jnp.sum(
        jnp.where(route_experts[:, :, None] == chosen, route_weights[:, :, None], 0.0), axis=1
    )
    expert_mix, shared_grad = mix(weights, mixed, folds, shared_rows)
    return (
        expert_mix[None],
        query_grad[None],
        rotary_grad[None],
        key_grad[None],
        value_grad[None],
        shared_grad[None],
    )


def solution(mesh):
    return jax.shard_map(
        per_device,
        mesh=mesh,
        in_specs=(
            P("section", "expert", None),
            P("section", "expert", None),
            P("section", "expert", None),
            P("section", "expert", None),
            P("section", None, "expert"),
            P("section", None, "expert"),
            P("section", "expert", None),
            P("section", None, "expert"),
            P("section", None, "expert"),
            P("section", None, "expert"),
            P("section", None, None),
            P("section", None, "expert"),
            P("section", None, "expert"),
        ),
        out_specs=(
            P("section", "expert", None),
            P("section", None, "expert"),
            P("section", None, "expert"),
            P("section", None, "expert"),
            P("section", None, "expert"),
            P("section", "expert", None),
        ),
        check_vma=False,
    )
```
